128 devices in a mesh: group: 8 (over x_lo, y), ctx: 16 (over z, x_hi, core).
Axes of the slice: x: 4 (x_hi: 2, x_lo: 2; x = x_hi * 2 + x_lo), y: 4, z: 4, core: 2. Of those that a mesh axis runs over, the one named last changes fastest.
Arguments:
- query_latent: bfloat16 [80, 2, 1536], P('group'), may hold values from -6 to 6
- w_query: bfloat16 [1536, 12288], P(None, 'ctx'), may hold values from -0.15625 to 0.15625
- w_key_up: bfloat16 [64, 128, 512], P('ctx'), may hold values from -0.5 to 0.5
- w_value_up: bfloat16 [64, 512, 128], P('ctx'), may hold values from -0.25 to 0.25
- cache: bfloat16 [16, 12288, 576], P('group', 'ctx'), may hold values from -1900 to 1900
- fresh: bfloat16 [8, 8, 12288, 576], P('group', None, 'ctx'), may hold values from -1900 to 1900, as said below
- new_latent: bfloat16 [80, 2, 576], P('group'), may hold values from -6 to 6
- lengths: int32 [80], P('group'), may hold values from 1 to 12288
- fresh_slot: int32 [8, 8], P('group'), may hold values from 0 to 7, each once within a row
- positions: int32 [80, 2], P('group'), may hold values from 0 to 65535
Outputs:
- attended: bfloat16 [80, 2, 8192], P('group', None, 'ctx')
The draws below stay inside these ranges and needn't reach their ends.
Inputs may be any that keep to these rules, and one draw needn't show every extreme that they name: `fresh`: latent cache entries. Each row of fresh_slot names every one of the 8 received slots once.
All inputs are finite; a program needn't handle non-finite values.
Results may differ from the reference program's by a relative error of at most 0.04.
Values may be sent and summed in bfloat16 or wider, within the bound.
No kernel may reach another device: no remote copies, remote signals or barrier semaphores. Data moves between devices by JAX's collectives and lax.ppermute only.
A program may use at most 128 MiB of HBM per device.

```python
import jax
import jax.numpy as jnp
from jax import lax

H = 64
LAT = 512
ROPE = 64
NOPE = 128
VDIM = 128
QLAT = 1536
RES = 2
NEWQ = 1
FRESH = 8
ROWS_G = 10
ROWS = 80
RES_ALL = 16
CTX = 12288
N_GROUP = 8


def spiky_cache(key, shape, chance, factor):
    first_key, second_key, third_key, fourth_key = jax.random.split(key, 4)
    base = jax.random.normal(first_key, shape, jnp.float32)
    marked = jax.random.bernoulli(second_key, chance, shape[:-1])
    strength = factor * jax.random.uniform(fourth_key, shape[:-1], jnp.float32, 0.5, 1.5)
    column = jnp.arange(shape[-1], dtype=jnp.int32)
    rotary = (column >= LAT).astype(jnp.float32)
    boost = 1.0 + (strength * marked.astype(jnp.float32))[..., None] * rotary
    large = base * boost
    after = jnp.roll(marked, 1, axis=-1)
    twin = jnp.roll(large, 1, axis=-2) + jax.random.normal(third_key, shape, jnp.float32)
    return jnp.where(after[..., None], twin, large)


def draw_cache(key, part):
    key = jax.random.fold_in(key, 11)
    shape = (RES_ALL, CTX, LAT + ROPE)
    values = spiky_cache(key, shape, 0.0, 0.0)
    return values.astype(jnp.bfloat16)


def draw_fresh(key, part):
    key = jax.random.fold_in(key, 23)
    shape = (N_GROUP, FRESH, CTX, LAT + ROPE)
    values = spiky_cache(key, shape, 0.0, 0.0)
    return values.astype(jnp.bfloat16)


def place_ends(drawn, key, low, top_value):
    dims = drawn.shape
    index_at = [jax.random.randint(jax.random.fold_in(key, axis), (), 0, dims[axis]) for axis in range(len(dims))]
    drawn = drawn.at[tuple(index_at)].set(low)
    longest = dims.index(max(dims))
    index_at[longest] = (index_at[longest] + 1) % dims[longest]
    return drawn.at[tuple(index_at)].set(top_value)


def steps_of(stream_key, dims, pieces, low, high):
    gain = 1.0
    for position, shards_of in pieces:
        draws = jax.random.uniform(jax.random.fold_in(jax.random.fold_in(stream_key, 6), position), (shards_of,), jnp.float32, low / len(pieces), high / len(pieces))
        gain = gain * jnp.repeat(jnp.exp(draws), dims[position] // shards_of).reshape((-1,) + (1,) * (len(dims) - 1 - position))
    return gain


def gaussian(stream_key, extent, spread, most, pieces=(), kind=jnp.bfloat16):
    drawn = jax.random.normal(stream_key, extent, jnp.float32) * spread
    if len(pieces) > 0:
        drawn = steps_of(stream_key, extent, pieces, -0.22, 0.18) * drawn
    return jnp.clip(drawn, min=-most, max=most).astype(kind)


def setup_inputs(seed: int = 0) -> dict:
    seeds = jax.random.split(jax.random.key(seed), 11)
    return {
        "query_latent": gaussian(seeds[0], (ROWS, 2, QLAT), 1.0, 6.0, ((0, 8),)),
        "w_query": gaussian(seeds[1], (QLAT, H * (NOPE + ROPE)), QLAT ** -0.5, 0.15625, ((1, 16),)),
        "w_key_up": gaussian(seeds[2], (H, NOPE, LAT), NOPE ** -0.5, 0.5, ((0, 16),)),
        "w_value_up": gaussian(seeds[3], (H, LAT, VDIM), LAT ** -0.5, 0.25, ((0, 16),)),
        "cache": draw_cache(jax.random.fold_in(seeds[10], 71), 0),
        "fresh": draw_fresh(jax.random.fold_in(seeds[10], 71), 0),
        "new_latent": gaussian(seeds[6], (ROWS, 2, LAT + ROPE), 1.0, 6.0, ((0, 8),)),
        "lengths": place_ends(jax.random.randint(seeds[7], (ROWS,), 1, CTX + 1), jax.random.fold_in(seeds[7], 1), 1, CTX).astype(jnp.int32),
        "fresh_slot": jax.vmap(lambda own: jax.random.permutation(own, FRESH))(jax.random.split(seeds[8], N_GROUP)).reshape((N_GROUP, FRESH)).astype(jnp.int32),
        "positions": place_ends(jax.random.randint(seeds[9], (ROWS, 2), 0, 65536), jax.random.fold_in(seeds[9], 1), 0, 65535).astype(jnp.int32),
    }


def rotate(values, where_at):
    half = values.shape[-1] // 2
    freqs = 50000.0 ** (-jnp.arange(half, dtype=jnp.float32) / half)
    angles = where_at.astype(jnp.float32)[..., None] * freqs
    cosine = jnp.cos(angles)
    sine = jnp.sin(angles)
    first = values[..., :half]
    second = values[..., half:]
    return jnp.concatenate([first * cosine - second * sine, second * cosine + first * sine], -1)


def reference(query_latent, w_query, w_key_up, w_value_up, cache, fresh, new_latent, lengths, fresh_slot, positions):
    score_scale = (NOPE + ROPE) ** -0.5
    qfull = jnp.dot(query_latent.reshape(ROWS * 2, QLAT), w_query, preferred_element_type=jnp.float32)
    qfull = qfull.astype(jnp.bfloat16).reshape(ROWS, 2, H, NOPE + ROPE)
    latent_query = jnp.einsum("rshn,hnl->rshl", qfull[..., :NOPE].astype(jnp.float32), w_key_up.astype(jnp.float32))
    rotated = rotate(qfull[..., NOPE:].astype(jnp.float32), positions[:, :, None])
    q_abs = jnp.concatenate([latent_query, rotated], -1).astype(jnp.bfloat16)
    new_keys = jnp.concatenate([new_latent[..., :LAT].astype(jnp.float32), rotate(new_latent[..., LAT:].astype(jnp.float32), positions)], -1).astype(jnp.bfloat16)
    step_of = jnp.arange(2 * H, dtype=jnp.int32) // H
    allowed = jnp.arange(2, dtype=jnp.int32)[None, :] <= step_of[:, None]

    def one_row(row):
        group_id = row // ROWS_G
        inside = row % ROWS_G
        resident_keys = cache[group_id * RES + jnp.minimum(inside, RES - 1)]
        slot = fresh_slot[group_id, jnp.maximum(inside - RES, 0)]
        fresh_keys = fresh[slot // NEWQ, group_id * NEWQ + slot % NEWQ]
        keys = jnp.where(inside < RES, resident_keys, fresh_keys)
        queries = q_abs[row].reshape(2 * H, LAT + ROPE)
        scores = jnp.dot(queries, keys.T, preferred_element_type=jnp.float32) * score_scale
        live = jnp.arange(CTX, dtype=jnp.int32)[None, :] < lengths[row]
        scores = jnp.where(live, scores, -1e30)
        own_keys = new_keys[row]
        new_scores = jnp.dot(queries, own_keys.T, preferred_element_type=jnp.float32) * score_scale
        new_scores = jnp.where(allowed, new_scores, -1e30)
        highest = jnp.maximum(jnp.max(scores, -1), jnp.max(new_scores, -1))
        weights = jnp.where(live, jnp.exp(scores - highest[:, None]), 0.0)
        new_weights = jnp.where(allowed, jnp.exp(new_scores - highest[:, None]), 0.0)
        total = jnp.sum(weights, -1) + jnp.sum(new_weights, -1)
        summed = jnp.dot(weights.astype(jnp.bfloat16), keys[:, :LAT], preferred_element_type=jnp.float32)
        summed = summed + jnp.dot(new_weights.astype(jnp.bfloat16), own_keys[:, :LAT], preferred_element_type=jnp.float32)
        return (summed / total[:, None]).astype(jnp.bfloat16).reshape(2, H, LAT)

    latent_out = lax.map(one_row, jnp.arange(ROWS, dtype=jnp.int32))
    attended = jnp.einsum("rshl,hlv->rshv", latent_out.astype(jnp.float32), w_value_up.astype(jnp.float32))
    return attended.astype(jnp.bfloat16).reshape(ROWS, 2, H * VDIM)
```

```python
import functools
import math

import jax
import jax.numpy as jnp
import numpy as np
from jax import lax
from jax.experimental import pallas as pl
from jax.experimental.pallas import tpu as pltpu
from jax.sharding import Mesh
from jax.sharding import PartitionSpec as P

LAT = 512
ROPE = 64
NOPE = 128
HEAD = NOPE + ROPE
WIDE = 640
SCALE = HEAD ** (-0.5)
NONE = -1e30
BF = jnp.bfloat16
F32 = jnp.float32

HALF_PI = (1.5703125, 0.0004825592041015625, 1.2676710047e-06)


def dot(a, b, contract=((1,), (0,))):
    return lax.dot_general(a, b, (contract, ((), ())), preferred_element_type=F32)


def iota(shape, dim):
    return lax.broadcasted_iota(jnp.int32, shape, dim)


def cos_sin(angle):
    turns = jnp.floor(angle * (2.0 / math.pi) + 0.5)
    rest = angle - turns * HALF_PI[0]
    rest = rest - turns * HALF_PI[1]
    rest = rest - turns * HALF_PI[2]
    sq = rest * rest
    sine = rest + rest * sq * (
        -1.6666654611e-1 + sq * (8.3321608736e-3 + sq * -1.9515295891e-4)
    )
    cosine = 1.0 - 0.5 * sq + sq * sq * (
        4.166664568298827e-2 + sq * (-1.388731625493765e-3 + sq * 2.443315711809948e-5)
    )
    quarter = turns.astype(jnp.int32) & 3
    swapped = (quarter & 1) == 1
    first = jnp.where(swapped, sine, cosine)
    second = jnp.where(swapped, cosine, sine)
    first = jnp.where((quarter == 1) | (quarter == 2), -first, first)
    second = jnp.where(quarter >= 2, -second, second)
    return first, second


def rope(values, cosine, signed_sine):
    half = ROPE // 2
    swapped = jnp.concatenate([values[:, half:], values[:, :half]], 1)
    return values * cosine + swapped * signed_sine


def per_row(ref, rows, width):
    count = 32
    at = iota((count, 1), 0)
    out = jnp.zeros((count, 1), jnp.int32)
    for r in range(rows):
        if width is None:
            out = jnp.where(at // 2 == r, ref[r], out)
        else:
            for s in range(width):
                out = jnp.where(at == r * width + s, ref[r, s], out)
    return out


def angles_of(pos_ref, freq_ref, rows):
    at = per_row(pos_ref, rows, 2).astype(F32)
    cosine, sine = cos_sin(at * freq_ref[...])
    signed = jnp.where(iota((1, ROPE), 1) < ROPE // 2, -1.0, 1.0) * sine
    return cosine, signed


def row_of(slot_ref, slots, resident, shape, dim, per):
    at = iota(shape, dim)
    slot = at // per
    out = slot - slots
    for j in range(slots):
        out = jnp.where(slot == slot_ref[0, j], resident + j, out)
    return out


def project_kernel(heads, slots, copies, slot_ref, len_ref, pos_ref, ql_ref, wq_ref, wk_ref, freq_ref,
                   out_ref, res_ref, own_ref, rows_ref, all_ref):
    rows = ql_ref.shape[0]
    resident = rows - slots
    rows_ref[...] = jnp.zeros_like(rows_ref)
    for r in range(rows):
        rows_ref[2 * r : 2 * r + 2, :] = ql_ref[r].astype(F32)
    qfull = dot(rows_ref[...].astype(BF), wq_ref[...]).astype(BF)
    cosine, signed = angles_of(pos_ref, freq_ref, rows)
    length = per_row(len_ref, rows, None)
    lane = iota((1, WIDE - LAT - ROPE), 1)
    meta = jnp.where(lane == 0, (length // 128).astype(F32), jnp.where(lane == 1, (length % 128).astype(F32), 0.0))
    for h in range(heads):
        part = qfull[:, h * HEAD : (h + 1) * HEAD]
        all_ref[h * 32 : (h + 1) * 32, :LAT] = dot(part[:, :NOPE], wk_ref[h]).astype(BF)
        tail = jnp.concatenate([rope(part[:, NOPE:].astype(F32), cosine, signed), meta], 1)
        all_ref[h * 32 : (h + 1) * 32, LAT:] = tail.astype(BF)
    piece = 2 * heads
    count = rows * piece
    row = row_of(slot_ref, slots, resident, (count, 1), 0, piece)
    inner = iota((count, 1), 0) % piece
    source = (inner // 2) * 32 + 2 * row + inner % 2
    select = jnp.where(iota((count, heads * 32), 1) == source, 1.0, 0.0).astype(BF)
    own = dot(select, all_ref[...])
    own_ref[...] = own.astype(BF)
    for p in range(slots):
        one = own[p * piece : (p + 1) * piece]
        two = jnp.concatenate([one, one], 0).astype(BF)
        for k in range(0, copies, 2):
            at = (p * copies + k) * piece
            out_ref[at : at + 2 * piece, :] = two
    last = own[slots * piece :].astype(BF)
    for k in range(copies):
        at = k * resident * piece
        res_ref[at : at + resident * piece, :] = last


def own_keys_kernel(slots, slot_ref, pos_ref, nl_ref, freq_ref, own_ref, out_ref, stat_ref, keys_ref):
    rows = nl_ref.shape[0]
    resident = rows - slots
    count = own_ref.shape[0]
    piece = count // rows
    keys_ref[...] = jnp.zeros_like(keys_ref)
    for r in range(rows):
        keys_ref[2 * r : 2 * r + 2, :] = nl_ref[r].astype(F32)
    cosine, signed = angles_of(pos_ref, freq_ref, rows)
    latent = keys_ref[:, :LAT].astype(BF)
    turned = rope(keys_ref[:, LAT:], cosine, signed).astype(BF)
    scores = dot(own_ref[:, :LAT], latent, ((1,), (1,)))
    scores = scores + dot(own_ref[:, LAT : LAT + ROPE], turned, ((1,), (1,)))
    scores = scores * SCALE
    row = row_of(slot_ref, slots, resident, (count, 1), 0, piece)
    step = iota((count, 1), 0) % 2
    key = iota((1, 32), 1)
    allowed = (key // 2 == row) & (key % 2 <= step)
    highest = jnp.max(jnp.where(allowed, scores, NONE), 1, keepdims=True)
    weights = jnp.where(allowed, jnp.exp(scores - highest), 0.0)
    total = jnp.sum(weights, 1, keepdims=True)
    out_ref[...] = dot(weights.astype(BF), latent)
    lane = iota((1, 128), 1)
    stat_ref[...] = jnp.where(lane == 0, highest, total)


def parts_of(value):
    first = value.astype(BF).astype(F32)
    second = (value - first).astype(BF).astype(F32)
    return first, second, value - first - second


def with_stats(highest, total):
    lane = iota((1, 128), 1)
    out = 0.0
    for at, part in enumerate(parts_of(highest) + parts_of(total)):
        out = jnp.where(lane == at, part, out)
    return out.astype(BF)


def stats_of(tail):
    tail = tail.astype(F32)
    highest = tail[:, 0:1] + tail[:, 1:2] + tail[:, 2:3]
    total = tail[:, 3:4] + tail[:, 4:5] + tail[:, 5:6]
    return highest, total


def attend(queries, keys, offset):
    length = queries[:, LAT + ROPE : LAT + ROPE + 2].astype(F32)
    length = (length[:, 0:1] * 128.0 + length[:, 1:2]).astype(jnp.int32)
    scores = dot(queries[:, : LAT + ROPE], keys, ((1,), (1,))) * SCALE
    live = iota((1, keys.shape[0]), 1) < length - offset
    highest = jnp.max(jnp.where(live, scores, NONE), 1, keepdims=True)
    weights = jnp.where(live, jnp.exp(scores - highest), 0.0)
    total = jnp.sum(weights, 1, keepdims=True)
    summed = dot(weights.astype(BF), keys[:, :LAT])
    return highest, total, summed / jnp.maximum(total, 1e-30)


def attend_new_kernel(offset_ref, own_ref, other_ref, keys_ref, send_ref, keep_ref, stat_ref):
    half = own_ref.shape[0]
    queries = jnp.concatenate([other_ref[...], own_ref[...]], 0)
    highest, total, mean = attend(queries, keys_ref[0], offset_ref[0])
    send_ref[:, :LAT] = mean[:half].astype(BF)
    send_ref[:, LAT:] = with_stats(highest[:half], total[:half])
    keep_ref[...] = mean[half:]
    lane = iota((1, 128), 1)
    stat_ref[...] = jnp.where(lane == 0, highest[half:], total[half:])


def attend_resident_kernel(piece, offset_ref, own_ref, other_ref, keys_ref, send_ref, keep_ref, stat_ref):
    rows = keys_ref.shape[0]
    half = own_ref.shape[0]
    copies = half // rows // piece
    lane = iota((1, 128), 1)
    results = []
    for i in range(rows):
        at = [(k * rows + i) * piece for k in range(copies)]
        queries = [ref[a : a + piece, :] for ref in (other_ref, own_ref) for a in at]
        results.append(attend(jnp.concatenate(queries, 0), keys_ref[i], offset_ref[0]))
    n = copies * piece
    for k in range(copies):
        parts = [tuple(x[k * piece : (k + 1) * piece] for x in one) for one in results]
        highest, total, mean = (jnp.concatenate(x, 0) for x in zip(*parts))
        span = slice(k * rows * piece, (k + 1) * rows * piece)
        send_ref[span, :LAT] = mean.astype(BF)
        send_ref[span, LAT:] = with_stats(highest, total)
        parts = [tuple(x[n + k * piece : n + (k + 1) * piece] for x in one) for one in results]
        highest, total, mean = (jnp.concatenate(x, 0) for x in zip(*parts))
        keep_ref[span, :] = mean
        stat_ref[span, :] = jnp.where(lane == 0, highest, total)


def join_kernel(got_ref, keep_ref, stat_ref, out_ref):
    far_highest, far_total = stats_of(got_ref[:, LAT:])
    highest, total = stat_ref[:, 0:1], stat_ref[:, 1:2]
    top = jnp.maximum(far_highest, highest)
    far_total = far_total * jnp.exp(far_highest - top)
    total = total * jnp.exp(highest - top)
    both = total + far_total
    scale = 1.0 / jnp.maximum(both, 1e-30)
    mean = got_ref[:, :LAT].astype(F32) * (far_total * scale) + keep_ref[...] * (total * scale)
    out_ref[:, :LAT] = mean.astype(BF)
    out_ref[:, LAT:] = with_stats(top, both)


def finish_kernel(slots, slot_ref, new_ref, res_ref, own_ref, stat_ref, wv_ref, out_ref):
    heads = wv_ref.shape[0]
    piece = 2 * heads
    rows = out_ref.shape[0]
    resident = rows - slots
    copies = new_ref.shape[0] // slots // piece

    def merged(ref, start, stride, n, own_at):
        spans = [slice(start + k * stride, start + k * stride + n) for k in range(copies)]
        stats = [stats_of(ref[s, LAT:]) for s in spans]
        stats.append((stat_ref[own_at : own_at + n, 0:1], stat_ref[own_at : own_at + n, 1:2]))
        top = functools.reduce(jnp.maximum, [h for h, _ in stats])
        fades = [jnp.exp(h - top) for h, _ in stats]
        total = sum(f * t for f, (_, t) in zip(fades, stats))
        summed = own_ref[own_at : own_at + n, :] * fades[-1]
        for s, f, (_, t) in zip(spans, fades, stats):
            summed = summed + ref[s, :LAT].astype(F32) * (f * t)
        return (summed / total).astype(BF)

    latent = [merged(new_ref, p * copies * piece, piece, piece, p * piece) for p in range(slots)]
    latent.append(merged(res_ref, 0, resident * piece, resident * piece, slots * piece))
    latent = jnp.concatenate(latent, 0)
    count = rows * piece
    inner = iota((count, 1), 0) % piece
    values = []
    for h in range(heads):
        one = dot(latent, wv_ref[h])
        values.append(jnp.where(inner // 2 == h, one, 0.0).astype(BF))
    values = jnp.concatenate(values, 1)
    row = row_of(slot_ref, slots, resident, (1, count), 1, piece)
    target = 2 * row + iota((1, count), 1) % 2
    select = jnp.where(iota((32, count), 0) == target, 1.0, 0.0).astype(BF)
    out = dot(select, values)
    for r in range(rows):
        out_ref[r] = out[2 * r : 2 * r + 2].astype(BF)


VMEM = pl.BlockSpec(memory_space=pltpu.VMEM)
SMEM = pl.BlockSpec(memory_space=pltpu.SMEM)


def shape(dims, dtype):
    return jax.ShapeDtypeStruct(dims, dtype)


def local(query_latent, w_query, w_key_up, w_value_up, cache, fresh, new_latent, lengths, fresh_slot, positions):
    rows, _, depth = query_latent.shape
    heads = w_key_up.shape[0]
    slots = fresh_slot.shape[1]
    resident = rows - slots
    tokens = cache.shape[1]
    copies = lax.axis_size("zx")
    piece = 2 * heads
    half = copies * piece
    params = pltpu.CompilerParams(vmem_limit_bytes=32 * 1024 * 1024)
    freqs = 50000.0 ** (-np.arange(ROPE // 2, dtype=np.float64) / (ROPE // 2))
    freqs = jnp.asarray(np.concatenate([freqs, freqs]).astype(np.float32)[None])
    offset = ((lax.axis_index("zx") * lax.axis_size("core") + lax.axis_index("core")) * tokens).reshape(1)

    out_q, res_q, own_q = pl.pallas_call(
        functools.partial(project_kernel, heads, slots, copies),
        out_shape=(
            shape((slots * half, WIDE), BF),
            shape((resident * half, WIDE), BF),
            shape((rows * piece, WIDE), BF),
        ),
        in_specs=[SMEM] * 3 + [VMEM] * 4,
        out_specs=[VMEM] * 3,
        scratch_shapes=[pltpu.VMEM((32, depth), F32), pltpu.VMEM((heads * 32, WIDE), BF)],
        compiler_params=params,
        name="project",
    )(fresh_slot, lengths, positions, query_latent, w_query, w_key_up, freqs)

    own_out, own_stat = pl.pallas_call(
        functools.partial(own_keys_kernel, slots),
        out_shape=(shape((rows * piece, LAT), F32), shape((rows * piece, 128), F32)),
        in_specs=[SMEM] * 2 + [VMEM] * 3,
        out_specs=[VMEM] * 2,
        scratch_shapes=[pltpu.VMEM((32, LAT + ROPE), F32)],
        compiler_params=params,
        name="own_keys",
    )(fresh_slot, positions, new_latent, freqs, own_q)

    def exchange(x, axes, n):
        return lax.all_to_all(x.reshape(n, -1, WIDE), axes, 0, 0, tiled=True).reshape(-1, WIDE)

    def swap(x):
        return lax.ppermute(x, "core", [(0, 1), (1, 0)])

    res_own = exchange(res_q, "zx", copies)
    new_own = exchange(out_q, ("group", "zx"), slots * copies)
    res_other = swap(res_own)
    new_other = swap(new_own)

    res_send, res_keep, res_stat = pl.pallas_call(
        functools.partial(attend_resident_kernel, piece),
        out_shape=(
            shape((resident * half, WIDE), BF),
            shape((resident * half, LAT), F32),
            shape((resident * half, 128), F32),
        ),
        in_specs=[SMEM] + [VMEM] * 3,
        out_specs=[VMEM] * 3,
        compiler_params=params,
        name="attend_resident",
    )(offset, res_own, res_other, cache)

    new_send, new_keep, new_stat = pl.pallas_call(
        attend_new_kernel,
        grid=(slots,),
        out_shape=(
            shape((slots * half, WIDE), BF),
            shape((slots * half, LAT), F32),
            shape((slots * half, 128), F32),
        ),
        in_specs=[
            SMEM,
            pl.BlockSpec((half, WIDE), lambda i: (i, 0)),
            pl.BlockSpec((half, WIDE), lambda i: (i, 0)),
            pl.BlockSpec((1, tokens, LAT + ROPE), lambda i: (i, 0, 0)),
        ],
        out_specs=[
            pl.BlockSpec((half, WIDE), lambda i: (i, 0)),
            pl.BlockSpec((half, LAT), lambda i: (i, 0)),
            pl.BlockSpec((half, 128), lambda i: (i, 0)),
        ],
        compiler_params=params,
        name="attend_new",
    )(offset, new_own, new_other, fresh[0])

    def join(got, keep, stat):
        return pl.pallas_call(
            join_kernel,
            out_shape=shape(got.shape, BF),
            in_specs=[VMEM] * 3,
            out_specs=VMEM,
            compiler_params=params,
            name="join_cores",
        )(got, keep, stat)

    res_back = exchange(join(swap(res_send), res_keep, res_stat), "zx", copies)
    new_back = exchange(join(swap(new_send), new_keep, new_stat), ("group", "zx"), slots * copies)

    return pl.pallas_call(
        functools.partial(finish_kernel, slots),
        out_shape=shape((rows, 2, heads * 128), BF),
        in_specs=[SMEM] + [VMEM] * 5,
        out_specs=VMEM,
        compiler_params=params,
        name="finish",
    )(fresh_slot, new_back, res_back, own_out, own_stat, w_value_up)


def solution(mesh):
    groups, shards = mesh.devices.shape
    split = Mesh(mesh.devices.reshape(groups, shards // 2, 2), ("group", "zx", "core"))
    ctx = ("zx", "core")
    placed = (
        P("group", None, None),
        P(None, ctx),
        P(ctx, None, None),
        P(ctx, None, None),
        P("group", ctx, None),
        P("group", None, ctx, None),
        P("group", None, None),
        P("group"),
        P("group", None),
        P("group", None),
    )
    return jax.shard_map(
        local, mesh=split, in_specs=placed, out_specs=P("group", None, ctx), check_vma=False
    )
```

```python
import functools
import math

import jax
import jax.numpy as jnp
import numpy as np
from jax import lax
from jax.experimental import pallas as pl
from jax.experimental.pallas import tpu as pltpu
from jax.sharding import Mesh
from jax.sharding import PartitionSpec as P

LAT = 512
ROPE = 64
NOPE = 128
HEAD = NOPE + ROPE
WIDE = 640
SCALE = HEAD ** (-0.5)
NONE = -1e30
BF = jnp.bfloat16
F32 = jnp.float32

HALF_PI = (1.5703125, 0.0004825592041015625, 1.2676710047e-06)


def dot(a, b, contract=((1,), (0,))):
    return lax.dot_general(a, b, (contract, ((), ())), preferred_element_type=F32)


def iota(shape, dim):
    return lax.broadcasted_iota(jnp.int32, shape, dim)


def cos_sin(angle):
    turns = jnp.floor(angle * (2.0 / math.pi) + 0.5)
    rest = angle - turns * HALF_PI[0]
    rest = rest - turns * HALF_PI[1]
    rest = rest - turns * HALF_PI[2]
    sq = rest * rest
    sine = rest + rest * sq * (
        -1.6666654611e-1 + sq * (8.3321608736e-3 + sq * -1.9515295891e-4)
    )
    cosine = 1.0 - 0.5 * sq + sq * sq * (
        4.166664568298827e-2 + sq * (-1.388731625493765e-3 + sq * 2.443315711809948e-5)
    )
    quarter = turns.astype(jnp.int32) & 3
    swapped = (quarter & 1) == 1
    first = jnp.where(swapped, sine, cosine)
    second = jnp.where(swapped, cosine, sine)
    first = jnp.where((quarter == 1) | (quarter == 2), -first, first)
    second = jnp.where(quarter >= 2, -second, second)
    return first, second


def rope(values, cosine, signed_sine):
    half = ROPE // 2
    swapped = jnp.concatenate([values[:, half:], values[:, :half]], 1)
    return values * cosine + swapped * signed_sine


def per_row(get, rows, width):
    at = iota((32, 1), 0)
    out = jnp.zeros((32, 1), jnp.int32)
    for r in range(rows):
        for s in range(width):
            out = jnp.where(at // (2 // width) == r * width + s, get(r, s), out)
    return out


def angles_of(pos_ref, freq_ref, rows):
    at = per_row(lambda r, s: pos_ref[s, r], rows, 2).astype(F32)
    cosine, sine = cos_sin(at * freq_ref[...])
    signed = jnp.where(iota((1, ROPE), 1) < ROPE // 2, -1.0, 1.0) * sine
    return cosine, signed


def row_of(slot_ref, slots, resident, shape, dim, per):
    at = iota(shape, dim)
    slot = at // per
    out = slot - slots
    for j in range(slots):
        out = jnp.where(slot == slot_ref[0, j], resident + j, out)
    return out


def project_kernel(heads, slots, copies, slot_ref, len_ref, pos_ref, ql_ref, wq_hbm, wk_hbm, freq_ref,
                   out_ref, res_ref, own_ref, rows_ref, all_ref, wq_ref, wk_ref, sems):
    rows = ql_ref.shape[0]
    resident = rows - slots
    chunks = wq_ref.shape[0]
    step = wq_ref.shape[1]
    loads = [
        pltpu.make_async_copy(wq_hbm.at[pl.ds(c * step, step)], wq_ref.at[c], sems.at[c]) for c in range(chunks)
    ]
    loads.append(pltpu.make_async_copy(wk_hbm, wk_ref, sems.at[chunks]))
    for load in loads:
        load.start()
    rows_ref[...] = jnp.zeros_like(rows_ref)
    for r in range(rows):
        rows_ref[2 * r : 2 * r + 2, :] = ql_ref[r].astype(F32)
    cosine, signed = angles_of(pos_ref, freq_ref, rows)
    length = per_row(lambda r, s: len_ref[r], rows, 1)
    lane = iota((1, WIDE - LAT - ROPE), 1)
    meta = jnp.where(lane == 0, (length // 128).astype(F32), jnp.where(lane == 1, (length % 128).astype(F32), 0.0))
    piece = 2 * heads
    count = rows * piece
    row = row_of(slot_ref, slots, resident, (count, 1), 0, piece)
    inner = iota((count, 1), 0) % piece
    source = (inner // 2) * 32 + 2 * row + inner % 2
    select = jnp.where(iota((count, heads * 32), 1) == source, 1.0, 0.0).astype(BF)
    qfull = 0.0
    for c in range(chunks):
        loads[c].wait()
        qfull = qfull + dot(rows_ref[:, c * step : (c + 1) * step].astype(BF), wq_ref[c])
    qfull = qfull.astype(BF)
    loads[chunks].wait()
    for h in range(heads):
        part = qfull[:, h * HEAD : (h + 1) * HEAD]
        all_ref[h * 32 : (h + 1) * 32, :LAT] = dot(part[:, :NOPE], wk_ref[h]).astype(BF)
        tail = jnp.concatenate([rope(part[:, NOPE:].astype(F32), cosine, signed), meta], 1)
        all_ref[h * 32 : (h + 1) * 32, LAT:] = tail.astype(BF)
    own = dot(select, all_ref[...])
    own_ref[...] = own.astype(BF)
    for p in range(slots):
        one = own[p * piece : (p + 1) * piece]
        two = jnp.concatenate([one, one], 0).astype(BF)
        for k in range(0, copies, 2):
            at = (p * copies + k) * piece
            out_ref[at : at + 2 * piece, :] = two
    res_ref[...] = own[slots * piece :].astype(BF)


def own_keys_kernel(slots, slot_ref, pos_ref, nl_ref, freq_ref, own_ref, out_ref, stat_ref, keys_ref):
    rows = nl_ref.shape[0]
    resident = rows - slots
    count = own_ref.shape[0]
    piece = count // rows
    keys_ref[...] = jnp.zeros_like(keys_ref)
    for r in range(rows):
        keys_ref[2 * r : 2 * r + 2, :] = nl_ref[r].astype(F32)
    cosine, signed = angles_of(pos_ref, freq_ref, rows)
    latent = keys_ref[:, :LAT].astype(BF)
    turned = rope(keys_ref[:, LAT:], cosine, signed).astype(BF)
    scores = dot(own_ref[:, :LAT], latent, ((1,), (1,)))
    scores = scores + dot(own_ref[:, LAT : LAT + ROPE], turned, ((1,), (1,)))
    scores = scores * SCALE
    row = row_of(slot_ref, slots, resident, (count, 1), 0, piece)
    step = iota((count, 1), 0) % 2
    key = iota((1, 32), 1)
    allowed = (key // 2 == row) & (key % 2 <= step)
    highest = jnp.max(jnp.where(allowed, scores, NONE), 1, keepdims=True)
    weights = jnp.where(allowed, jnp.exp(scores - highest), 0.0)
    total = jnp.sum(weights, 1, keepdims=True)
    out_ref[...] = dot(weights.astype(BF), latent)
    stat_ref[:, :128] = jnp.broadcast_to(highest, (count, 128))
    stat_ref[:, 128:] = jnp.broadcast_to(total, (count, 128))


def parts_of(value):
    first = value.astype(BF).astype(F32)
    second = (value - first).astype(BF).astype(F32)
    return first, second, value - first - second


def with_stats(highest, total):
    lane = iota((1, 128), 1)
    out = 0.0
    for at, part in enumerate(parts_of(highest) + parts_of(total)):
        out = jnp.where(lane == at, part, out)
    return out.astype(BF)


def stats_of(tail):
    at = iota((128, 256), 0)
    pick = jnp.where((at < 6) & (at // 3 == iota((128, 256), 1) // 128), 1.0, 0.0).astype(BF)
    both = dot(tail, pick)
    return both[:, :128], both[:, 128:]


def spread(value):
    return jnp.concatenate([value] * (LAT // 128), -1)


def softmax_part(scores, length):
    scores = jnp.where(iota((1, scores.shape[1]), 1) < length, scores, NONE)
    highest = jnp.max(scores, 1, keepdims=True)
    weights = jnp.exp((scores - jnp.maximum(highest, 0.1 * NONE)) * SCALE)
    return highest * SCALE, jnp.sum(weights, 1, keepdims=True), weights.astype(BF)


def attend_kernel(piece, offset_ref, fresh_hbm, cache_hbm, new_own, new_other, *refs):
    send_ref, keep_ref, stat_ref, keys_ref, sems = refs[-5:]
    blocks = refs[:-5]
    res_other, res_own = blocks[: len(blocks) // 2], blocks[len(blocks) // 2 :]
    slots, resident = fresh_hbm.shape[0], cache_hbm.shape[0]
    rows = slots + resident
    half = new_own.shape[0] // slots
    loads = [pltpu.make_async_copy(fresh_hbm.at[i], keys_ref.at[i], sems.at[i]) for i in range(slots)]
    loads += [
        pltpu.make_async_copy(cache_hbm.at[i], keys_ref.at[slots + i], sems.at[slots + i]) for i in range(resident)
    ]
    for load in loads:
        load.start()
    arrived = 0

    def queries_of(i):
        if i < slots:
            span = slice(i * half, (i + 1) * half)
            return jnp.concatenate([new_other[span, :], new_own[span, :]], 0)
        at = (i - slots) * piece
        step = resident * piece
        return jnp.concatenate(
            [ref[k + at : k + at + piece, :] for ref in res_other + res_own for k in range(0, ref.shape[0], step)], 0
        )

    def scores_of(i):
        queries = queries_of(i)
        length = queries[:, LAT + ROPE : LAT + ROPE + 2].astype(F32)
        length = (length[:, 0:1] * 128.0 + length[:, 1:2]).astype(jnp.int32) - offset_ref[0]
        return dot(queries[:, : LAT + ROPE], keys_ref[i]), length

    loads[0].wait()
    arrived = 1
    ahead = scores_of(0)
    for i in range(rows):
        scores, length = ahead
        if i + 1 < rows:
            if i + 1 == arrived:
                upto = min(rows, arrived + i + 2)
                for load in loads[arrived:upto]:
                    load.wait()
                arrived = upto
            ahead = scores_of(i + 1)
        highest, total, weights = softmax_part(scores, length)
        mean = dot(weights, keys_ref[i, :LAT, :], ((1,), (1,))) * (1.0 / jnp.maximum(total, 1e-30))
        stats = with_stats(highest, total)
        span = slice(i * half, (i + 1) * half)
        send_ref[span, :LAT] = mean[:half].astype(BF)
        send_ref[span, LAT:] = stats[:half]
        keep_ref[span, :] = mean[half:]
        stat_ref[span, :] = stats[half:]


def joined(got, keep, stat):
    far_highest, far_total = stats_of(got[:, LAT:])
    highest, total = stats_of(stat)
    top = jnp.maximum(far_highest, highest)
    far_total = far_total * jnp.exp(far_highest - top)
    total = total * jnp.exp(highest - top)
    both = total + far_total
    scale = 1.0 / jnp.maximum(both, 1e-30)
    mean = got[:, :LAT].astype(F32) * spread(far_total * scale) + keep * spread(total * scale)
    return mean.astype(BF), with_stats(top, both)


def join_kernel(slots, piece, got_ref, keep_ref, stat_ref, new_ref, *res_refs):
    mean, stats = joined(got_ref[...], keep_ref[...], stat_ref[...])
    count = new_ref.shape[0]
    half = count // slots
    new_ref[:, :LAT] = mean[:count]
    new_ref[:, LAT:] = stats[:count]
    resident = got_ref.shape[0] // half - slots
    block = 0
    for ref in res_refs:
        for k in range(0, ref.shape[0], resident * piece):
            for i in range(resident):
                at = count + i * half + block * piece
                span = slice(k + i * piece, k + (i + 1) * piece)
                ref[span, :LAT] = mean[at : at + piece]
                ref[span, LAT:] = stats[at : at + piece]
            block += 1


def merged(means, tails, own, own_highest, own_total):
    copies, n = means.shape[:2]
    highest, total = (x.reshape(copies, n, 128) for x in stats_of(tails.reshape(copies * n, 128)))
    top = jnp.maximum(jnp.max(highest, 0), own_highest)
    share = total * jnp.exp(highest - top[None])
    own_fade = jnp.exp(own_highest - top)
    scale = 1.0 / (jnp.sum(share, 0) + own_total * own_fade)
    summed = own * spread(own_fade * scale)
    share = share * scale[None]
    for k in range(copies):
        summed = summed + means[k].astype(F32) * spread(share[k])
    return summed.astype(BF)


def finish_kernel(slots, slot_ref, new_ref, own_ref, stat_ref, wv_ref, *refs):
    out_ref = refs[-1]
    heads = wv_ref.shape[0]
    piece = 2 * heads
    rows = out_ref.shape[0]
    resident = rows - slots
    n = resident * piece
    copies = new_ref.shape[0] // slots // piece
    mine = copies // 2 + 1
    parts = [ref[:n, :] for ref in refs[:mine]] + [ref[n:, :] for ref in refs[mine:-1]]

    def own_of(at, n):
        return own_ref[at : at + n, :], stat_ref[at : at + n, :128], stat_ref[at : at + n, 128:]

    half = copies * piece
    latent = []
    for p in range(slots):
        block = new_ref[p * half : (p + 1) * half, :].reshape(copies, piece, WIDE)
        latent.append(merged(block[..., :LAT], block[..., LAT:], *own_of(p * piece, piece)))
    block = jnp.stack(parts)
    latent.append(merged(block[..., :LAT], block[..., LAT:], *own_of(slots * piece, resident * piece)))
    latent = jnp.concatenate(latent, 0)
    count = rows * piece
    inner = iota((count, 1), 0) % piece
    values = []
    for h in range(heads):
        one = dot(latent, wv_ref[h])
        values.append(jnp.where(inner // 2 == h, one, 0.0).astype(BF))
    values = jnp.concatenate(values, 1)
    row = row_of(slot_ref, slots, resident, (1, count), 1, piece)
    target = 2 * row + iota((1, count), 1) % 2
    select = jnp.where(iota((32, count), 0) == target, 1.0, 0.0).astype(BF)
    out = dot(select, values)
    for r in range(rows):
        out_ref[r] = out[2 * r : 2 * r + 2].astype(BF)


VMEM = pl.BlockSpec(memory_space=pltpu.VMEM)
SMEM = pl.BlockSpec(memory_space=pltpu.SMEM)
ANY = pl.BlockSpec(memory_space=pl.ANY)


def shape(dims, dtype):
    return jax.ShapeDtypeStruct(dims, dtype)


def params(mebibytes):
    return pltpu.CompilerParams(vmem_limit_bytes=mebibytes * 1024 * 1024)


def cost(flops, moved):
    return pl.CostEstimate(flops=flops, bytes_accessed=moved, transcendentals=0)


def local(query_latent, w_query, w_key_up, w_value_up, cache, fresh, new_latent, lengths, fresh_slot, positions):
    rows, _, depth = query_latent.shape
    heads = w_key_up.shape[0]
    slots = fresh_slot.shape[1]
    resident = rows - slots
    tokens = cache.shape[1]
    copies = lax.axis_size("zx")
    piece = 2 * heads
    half = copies * piece
    chunks = 4
    freqs = 50000.0 ** (-np.arange(ROPE // 2, dtype=np.float64) / (ROPE // 2))
    freqs = jnp.asarray(np.concatenate([freqs, freqs]).astype(np.float32)[None])
    place = lax.axis_index("zx")
    offset = ((place * lax.axis_size("core") + lax.axis_index("core")) * tokens).reshape(1)
    positions = positions.T
    cache = jnp.swapaxes(cache, 1, 2)
    fresh = jnp.swapaxes(fresh[0], 1, 2)

    def in_hbm(x):
        return pltpu.with_memory_space_constraint(x, pltpu.HBM)

    out_q, res_q, own_q = pl.pallas_call(
        functools.partial(project_kernel, heads, slots, copies),
        out_shape=(
            shape((slots * half, WIDE), BF),
            shape((resident * piece, WIDE), BF),
            shape((rows * piece, WIDE), BF),
        ),
        in_specs=[SMEM] * 3 + [VMEM, ANY, ANY, VMEM],
        out_specs=[VMEM] * 3,
        scratch_shapes=[
            pltpu.VMEM((32, depth), F32),
            pltpu.VMEM((heads * 32, WIDE), BF),
            pltpu.VMEM((chunks, depth // chunks, heads * HEAD), BF),
            pltpu.VMEM((heads, NOPE, LAT), BF),
            pltpu.SemaphoreType.DMA((chunks + 1,)),
        ],
        compiler_params=params(16),
        name="project",
    )(*map(in_hbm, (fresh_slot, lengths, positions, query_latent, w_query, w_key_up, freqs)))

    own_out, own_stat = pl.pallas_call(
        functools.partial(own_keys_kernel, slots),
        out_shape=(shape((rows * piece, LAT), F32), shape((rows * piece, 256), F32)),
        in_specs=[SMEM] * 2 + [VMEM] * 3,
        out_specs=[VMEM] * 2,
        scratch_shapes=[pltpu.VMEM((32, LAT + ROPE), F32)],
        compiler_params=params(32),
        name="own_keys",
    )(fresh_slot, positions, new_latent, freqs, own_q)

    def exchange(x, axes, n):
        return lax.all_to_all(x.reshape(n, -1, WIDE), axes, 0, 0, tiled=True).reshape(-1, WIDE)

    def swap(x):
        return lax.ppermute(x, "core", [(0, 1), (1, 0)])

    def turned(x, k, sign):
        pairs = []
        for i in range(copies):
            pairs += [(2 * i, 2 * ((i + sign * k) % copies)), (2 * i + 1, 2 * ((i - sign * k) % copies) + 1)]
        return lax.ppermute(x, ("zx", "core"), pairs)

    new_own = exchange(out_q, ("group", "zx"), slots * copies)
    res_sib = swap(res_q)
    res_both = jnp.concatenate([res_q, res_sib], 0)
    near = [turned(res_both, k, 1) for k in range(1, copies // 2)]
    across = turned(res_q, copies // 2, 1)
    new_own, across, *near = lax.optimization_barrier((new_own, across, *near))
    new_other, across_sib, *far = map(swap, (new_own, across, *near))

    send, keep, stat = pl.pallas_call(
        functools.partial(attend_kernel, piece),
        out_shape=(shape((rows * half, WIDE), BF), shape((rows * half, LAT), F32), shape((rows * half, 128), BF)),
        in_specs=[SMEM] + [ANY] * 2 + [VMEM] * (4 + copies),
        out_specs=[VMEM] * 3,
        scratch_shapes=[pltpu.VMEM((rows, LAT + ROPE, tokens), BF), pltpu.SemaphoreType.DMA((rows,))],
        compiler_params=params(24),
        cost_estimate=cost(rows * 5 * 10**8, rows * 2 * 10**6),
        name="attend",
    )(offset, in_hbm(fresh), in_hbm(cache), new_own, new_other, *far, res_sib, across_sib, *near, res_q, across)

    new_part, *res_parts = pl.pallas_call(
        functools.partial(join_kernel, slots, piece),
        out_shape=(shape((slots * half, WIDE), BF),)
        + (shape((2 * resident * piece, WIDE), BF),) * len(near)
        + (shape((resident * piece, WIDE), BF),) * 2,
        in_specs=[VMEM] * 3,
        out_specs=(VMEM,) * (len(near) + 3),
        compiler_params=params(32),
        name="join_cores",
    )(swap(send), keep, stat)
    new_back = exchange(new_part, ("group", "zx"), slots * copies)
    *near, res_here, across = res_parts
    near = [turned(x, k + 1, -1) for k, x in enumerate(near)]
    across = turned(across, copies // 2, -1)
    res_back = [res_here, across, *near, *map(swap, near)]

    return pl.pallas_call(
        functools.partial(finish_kernel, slots),
        out_shape=shape((rows, 2, heads * 128), BF),
        in_specs=[SMEM] + [VMEM] * (4 + len(res_back)),
        out_specs=VMEM,
        compiler_params=params(32),
        name="finish",
    )(fresh_slot, new_back, own_out, own_stat, w_value_up, *res_back)


def solution(mesh):
    groups, shards = mesh.devices.shape
    split = Mesh(mesh.devices.reshape(groups, shards // 2, 2), ("group", "zx", "core"))
    ctx = ("zx", "core")
    placed = (
        P("group", None, None),
        P(None, ctx),
        P(ctx, None, None),
        P(ctx, None, None),
        P("group", ctx, None),
        P("group", None, ctx, None),
        P("group", None, None),
        P("group"),
        P("group", None),
        P("group", None),
    )
    return jax.shard_map(
        local, mesh=split, in_specs=placed, out_specs=P("group", None, ctx), check_vma=False
    )
```

```python
import functools
import math

import jax
import jax.numpy as jnp
import numpy as np
from jax import lax
from jax.experimental import pallas as pl
from jax.experimental.pallas import tpu as pltpu
from jax.sharding import Mesh
from jax.sharding import PartitionSpec as P

LAT = 512
ROPE = 64
NOPE = 128
HEAD = NOPE + ROPE
WIDE = 640
SCALE = HEAD ** (-0.5)
NONE = -1e30
BF = jnp.bfloat16
F32 = jnp.float32

HALF_PI = (1.5703125, 0.0004825592041015625, 1.2676710047e-06)


def dot(a, b, contract=((1,), (0,))):
    return lax.dot_general(a, b, (contract, ((), ())), preferred_element_type=F32)


def iota(shape, dim):
    return lax.broadcasted_iota(jnp.int32, shape, dim)


def cos_sin(angle):
    turns = jnp.floor(angle * (2.0 / math.pi) + 0.5)
    rest = angle - turns * HALF_PI[0]
    rest = rest - turns * HALF_PI[1]
    rest = rest - turns * HALF_PI[2]
    sq = rest * rest
    sine = rest + rest * sq * (
        -1.6666654611e-1 + sq * (8.3321608736e-3 + sq * -1.9515295891e-4)
    )
    cosine = 1.0 - 0.5 * sq + sq * sq * (
        4.166664568298827e-2 + sq * (-1.388731625493765e-3 + sq * 2.443315711809948e-5)
    )
    quarter = turns.astype(jnp.int32) & 3
    swapped = (quarter & 1) == 1
    first = jnp.where(swapped, sine, cosine)
    second = jnp.where(swapped, cosine, sine)
    first = jnp.where((quarter == 1) | (quarter == 2), -first, first)
    second = jnp.where(quarter >= 2, -second, second)
    return first, second


def rope(values, cosine, signed_sine):
    half = ROPE // 2
    swapped = jnp.concatenate([values[:, half:], values[:, :half]], 1)
    return values * cosine + swapped * signed_sine


def per_row(get, rows, width):
    at = iota((32, 1), 0)
    out = jnp.zeros((32, 1), jnp.int32)
    for r in range(rows):
        for s in range(width):
            out = jnp.where(at // (2 // width) == r * width + s, get(r, s), out)
    return out


def angles_of(pos_ref, freq_ref, rows):
    at = per_row(lambda r, s: pos_ref[s, r], rows, 2).astype(F32)
    cosine, sine = cos_sin(at * freq_ref[...])
    signed = jnp.where(iota((1, ROPE), 1) < ROPE // 2, -1.0, 1.0) * sine
    return cosine, signed


def row_of(slot_ref, slots, resident, shape, dim, per):
    at = iota(shape, dim)
    slot = at // per
    out = slot - slots
    for j in range(slots):
        out = jnp.where(slot == slot_ref[0, j], resident + j, out)
    return out


def project_kernel(heads, slots, copies, slot_hbm, len_hbm, pos_hbm, ql_hbm, wq_hbm, wk_hbm, freq_hbm,
                   out_ref, res_ref, own_ref, rows_ref, all_ref, slot_ref, len_ref, pos_ref, ql_ref, wq_ref, wk_ref,
                   freq_ref, sems):
    rows = ql_ref.shape[0]
    resident = rows - slots
    chunks = wq_ref.shape[0]
    step = wq_ref.shape[1]
    small = ((ql_hbm, ql_ref), (slot_hbm, slot_ref), (len_hbm, len_ref), (pos_hbm, pos_ref), (freq_hbm, freq_ref))
    small = [pltpu.make_async_copy(*pair, sems.at[chunks + 1 + n]) for n, pair in enumerate(small)]
    loads = [
        pltpu.make_async_copy(wq_hbm.at[pl.ds(c * step, step)], wq_ref.at[c], sems.at[c]) for c in range(chunks)
    ]
    loads.append(pltpu.make_async_copy(wk_hbm, wk_ref, sems.at[chunks]))
    for load in small + loads:
        load.start()
    for load in small:
        load.wait()
    rows_ref[...] = jnp.zeros_like(rows_ref)
    for r in range(rows):
        rows_ref[2 * r : 2 * r + 2, :] = ql_ref[r].astype(F32)
    cosine, signed = angles_of(pos_ref, freq_ref, rows)
    length = per_row(lambda r, s: len_ref[r], rows, 1)
    lane = iota((1, WIDE - LAT - ROPE), 1)
    meta = jnp.where(lane == 0, (length // 128).astype(F32), jnp.where(lane == 1, (length % 128).astype(F32), 0.0))
    piece = 2 * heads
    count = rows * piece
    row = row_of(slot_ref, slots, resident, (count, 1), 0, piece)
    inner = iota((count, 1), 0) % piece
    source = (inner // 2) * 32 + 2 * row + inner % 2
    select = jnp.where(iota((count, heads * 32), 1) == source, 1.0, 0.0).astype(BF)
    qfull = 0.0
    for c in range(chunks):
        loads[c].wait()
        qfull = qfull + dot(rows_ref[:, c * step : (c + 1) * step].astype(BF), wq_ref[c])
    qfull = qfull.astype(BF)
    loads[chunks].wait()
    for h in range(heads):
        part = qfull[:, h * HEAD : (h + 1) * HEAD]
        all_ref[h * 32 : (h + 1) * 32, :LAT] = dot(part[:, :NOPE], wk_ref[h]).astype(BF)
        tail = jnp.concatenate([rope(part[:, NOPE:].astype(F32), cosine, signed), meta], 1)
        all_ref[h * 32 : (h + 1) * 32, LAT:] = tail.astype(BF)
    own = dot(select, all_ref[...])
    own_ref[...] = own.astype(BF)
    for p in range(slots):
        one = own[p * piece : (p + 1) * piece]
        two = jnp.concatenate([one, one], 0).astype(BF)
        for k in range(0, copies, 2):
            at = (p * copies + k) * piece
            out_ref[at : at + 2 * piece, :] = two
    res_ref[...] = own[slots * piece :].astype(BF)


def own_keys_kernel(slots, slot_ref, pos_ref, nl_ref, freq_ref, own_ref, out_ref, stat_ref, order_ref, keys_ref):
    rows = nl_ref.shape[0]
    resident = rows - slots
    count = own_ref.shape[0]
    piece = count // rows
    keys_ref[...] = jnp.zeros_like(keys_ref)
    for r in range(rows):
        keys_ref[2 * r : 2 * r + 2, :] = nl_ref[r].astype(F32)
    cosine, signed = angles_of(pos_ref, freq_ref, rows)
    latent = keys_ref[:, :LAT].astype(BF)
    turned = rope(keys_ref[:, LAT:], cosine, signed).astype(BF)
    scores = dot(own_ref[:, :LAT], latent, ((1,), (1,)))
    scores = scores + dot(own_ref[:, LAT : LAT + ROPE], turned, ((1,), (1,)))
    scores = scores * SCALE
    row = row_of(slot_ref, slots, resident, (count, 1), 0, piece)
    step = iota((count, 1), 0) % 2
    key = iota((1, 32), 1)
    allowed = (key // 2 == row) & (key % 2 <= step)
    highest = jnp.max(jnp.where(allowed, scores, NONE), 1, keepdims=True)
    weights = jnp.where(allowed, jnp.exp(scores - highest), 0.0)
    total = jnp.sum(weights, 1, keepdims=True)
    out_ref[...] = dot(weights.astype(BF), latent)
    stat_ref[:, :128] = jnp.broadcast_to(highest, (count, 128))
    stat_ref[:, 128:] = jnp.broadcast_to(total, (count, 128))
    row = row_of(slot_ref, slots, resident, (1, count), 1, piece)
    target = 2 * row + iota((1, count), 1) % 2
    order_ref[...] = jnp.where(iota((32, count), 0) == target, 1.0, 0.0).astype(BF)


def parts_of(value):
    first = value.astype(BF).astype(F32)
    second = (value - first).astype(BF).astype(F32)
    return first, second, value - first - second


def with_stats(highest, total):
    lane = iota((1, 128), 1)
    out = 0.0
    for at, part in enumerate(parts_of(highest) + parts_of(total)):
        out = jnp.where(lane == at, part, out)
    return out.astype(BF)


def stats_of(tail):
    at = iota((128, 256), 0)
    pick = jnp.where((at < 6) & (at // 3 == iota((128, 256), 1) // 128), 1.0, 0.0).astype(BF)
    both = dot(tail, pick)
    return both[:, :128], both[:, 128:]


def spread(value):
    return jnp.concatenate([value] * (LAT // 128), -1)


def softmax_part(scores, length):
    scores = jnp.where(iota((1, scores.shape[1]), 1) < length, scores, NONE)
    highest = jnp.max(scores, 1, keepdims=True)
    weights = jnp.exp((scores - jnp.maximum(highest, 0.1 * NONE)) * SCALE)
    return highest * SCALE, jnp.sum(weights, 1, keepdims=True), weights.astype(BF)


def attend_kernel(piece, fresh_hbm, cache_ref, new_own, new_other, *refs):
    send_ref, keep_ref, stat_ref, keys_ref, sems = refs[-5:]
    blocks = refs[:-5]
    res_other, res_own = blocks[: len(blocks) // 2], blocks[len(blocks) // 2 :]
    slots, resident = fresh_hbm.shape[0], cache_ref.shape[0]
    rows = slots + resident
    half = new_own.shape[0] // slots
    loads = [pltpu.make_async_copy(fresh_hbm.at[i], keys_ref.at[i], sems.at[i]) for i in range(slots)]
    for load in loads:
        load.start()
    offset = (lax.axis_index("zx") * lax.axis_size("core") + lax.axis_index("core")) * keys_ref.shape[2]

    def queries_of(i):
        if i < slots:
            span = slice(i * half, (i + 1) * half)
            return jnp.concatenate([new_other[span, :], new_own[span, :]], 0)
        at = (i - slots) * piece
        step = resident * piece
        return jnp.concatenate(
            [ref[k + at : k + at + piece, :] for ref in res_other + res_own for k in range(0, ref.shape[0], step)], 0
        )

    def keys_of(i):
        return keys_ref.at[i] if i < slots else cache_ref.at[i - slots]

    def scores_of(i):
        queries = queries_of(i)
        length = queries[:, LAT + ROPE : LAT + ROPE + 2].astype(F32)
        length = (length[:, 0:1] * 128.0 + length[:, 1:2]).astype(jnp.int32) - offset
        return dot(queries[:, : LAT + ROPE], keys_of(i)[...]), length

    order = [*range(slots, rows), *range(slots)]
    arrived = 0
    ahead = scores_of(order[0])
    for n, i in enumerate(order):
        scores, length = ahead
        if n + 1 < rows:
            if order[n + 1] == arrived:
                upto = min(slots, arrived + n + 1)
                for load in loads[arrived:upto]:
                    load.wait()
                arrived = upto
            ahead = scores_of(order[n + 1])
        highest, total, weights = softmax_part(scores, length)
        mean = dot(weights, keys_of(i)[:LAT, :], ((1,), (1,))) * (1.0 / jnp.maximum(total, 1e-30))
        stats = with_stats(highest, total)
        span = slice(i * half, (i + 1) * half)
        send_ref[span, :LAT] = mean[:half].astype(BF)
        send_ref[span, LAT:] = stats[:half]
        keep_ref[span, :] = mean[half:]
        stat_ref[span, :] = stats[half:]


def joined(got, keep, stat):
    far_highest, far_total = stats_of(got[:, LAT:])
    highest, total = stats_of(stat)
    top = jnp.maximum(far_highest, highest)
    far_total = far_total * jnp.exp(far_highest - top)
    total = total * jnp.exp(highest - top)
    both = total + far_total
    scale = 1.0 / jnp.maximum(both, 1e-30)
    mean = got[:, :LAT].astype(F32) * spread(far_total * scale) + keep * spread(total * scale)
    return mean.astype(BF), with_stats(top, both)


def join_kernel(slots, piece, got_ref, keep_ref, stat_ref, new_hbm, *refs):
    res_refs, new_ref, sems = refs[:-2], refs[-2], refs[-1]
    count = new_ref.shape[0]
    half = count // slots
    resident = got_ref.shape[0] // half - slots
    parts = sems.shape[0]
    stores = []
    for c in range(parts):
        span = slice(c * count // parts, (c + 1) * count // parts)
        mean, stats = joined(got_ref[span, :], keep_ref[span, :], stat_ref[span, :])
        new_ref[span, :LAT] = mean
        new_ref[span, LAT:] = stats
        at = pl.ds(c * count // parts, count // parts)
        stores.append(pltpu.make_async_copy(new_ref.at[at], new_hbm.at[at], sems.at[c]))
        stores[c].start()
    mean, stats = joined(got_ref[count:, :], keep_ref[count:, :], stat_ref[count:, :])
    block = 0
    for ref in res_refs:
        for k in range(0, ref.shape[0], resident * piece):
            for i in range(resident):
                at = i * half + block * piece
                span = slice(k + i * piece, k + (i + 1) * piece)
                ref[span, :LAT] = mean[at : at + piece]
                ref[span, LAT:] = stats[at : at + piece]
            block += 1
    for store in stores:
        store.wait()


def merged(means, tails, own, own_highest, own_total):
    copies, n = means.shape[:2]
    highest, total = (x.reshape(copies, n, 128) for x in stats_of(tails.reshape(copies * n, 128)))
    top = jnp.maximum(jnp.max(highest, 0), own_highest)
    share = total * jnp.exp(highest - top[None])
    own_fade = jnp.exp(own_highest - top)
    scale = 1.0 / (jnp.sum(share, 0) + own_total * own_fade)
    summed = own * spread(own_fade * scale)
    share = share * scale[None]
    for k in range(copies):
        summed = summed + means[k].astype(F32) * spread(share[k])
    return summed.astype(BF)


def finish_kernel(slots, order_ref, new_ref, own_ref, stat_ref, wv_ref, *refs):
    out_ref = refs[-1]
    heads = wv_ref.shape[0]
    piece = 2 * heads
    rows = out_ref.shape[0]
    resident = rows - slots
    n = resident * piece
    copies = new_ref.shape[0] // slots // piece
    mine = copies // 2 + 1
    far_ref = refs[mine]
    parts = [ref[:n, :] for ref in refs[:mine]] + [far_ref[k : k + n, :] for k in range(0, far_ref.shape[0], n)]

    def own_of(at, n):
        return own_ref[at : at + n, :], stat_ref[at : at + n, :128], stat_ref[at : at + n, 128:]

    half = copies * piece
    latent = []
    for p in range(slots):
        block = new_ref[p * half : (p + 1) * half, :].reshape(copies, piece, WIDE)
        latent.append(merged(block[..., :LAT], block[..., LAT:], *own_of(p * piece, piece)))
    block = jnp.stack(parts)
    latent.append(merged(block[..., :LAT], block[..., LAT:], *own_of(slots * piece, resident * piece)))
    latent = jnp.concatenate(latent, 0)
    count = rows * piece
    inner = iota((count, 1), 0) % piece
    values = []
    for h in range(heads):
        one = dot(latent, wv_ref[h])
        values.append(jnp.where(inner // 2 == h, one, 0.0).astype(BF))
    values = jnp.concatenate(values, 1)
    out = dot(order_ref[...], values)
    for r in range(rows):
        out_ref[r] = out[2 * r : 2 * r + 2].astype(BF)


VMEM = pl.BlockSpec(memory_space=pltpu.VMEM)
SMEM = pl.BlockSpec(memory_space=pltpu.SMEM)
ANY = pl.BlockSpec(memory_space=pl.ANY)


def shape(dims, dtype):
    return jax.ShapeDtypeStruct(dims, dtype)


def params(mebibytes):
    return pltpu.CompilerParams(vmem_limit_bytes=mebibytes * 1024 * 1024)


def cost(flops, moved):
    return pl.CostEstimate(flops=flops, bytes_accessed=moved, transcendentals=0)


def local(query_latent, w_query, w_key_up, w_value_up, cache, fresh, new_latent, lengths, fresh_slot, positions):
    rows, _, depth = query_latent.shape
    heads = w_key_up.shape[0]
    slots = fresh_slot.shape[1]
    resident = rows - slots
    tokens = cache.shape[1]
    copies = lax.axis_size("zx")
    piece = 2 * heads
    half = copies * piece
    chunks = 6
    freqs = 50000.0 ** (-np.arange(ROPE // 2, dtype=np.float64) / (ROPE // 2))
    freqs = jnp.asarray(np.concatenate([freqs, freqs]).astype(np.float32)[None])
    positions = positions.T
    cache = jnp.swapaxes(cache, 1, 2)
    fresh = jnp.swapaxes(fresh[0], 1, 2)

    def in_hbm(x):
        return pltpu.with_memory_space_constraint(x, pltpu.HBM)

    out_q, res_q, own_q = pl.pallas_call(
        functools.partial(project_kernel, heads, slots, copies),
        out_shape=(
            shape((slots * half, WIDE), BF),
            shape((resident * piece, WIDE), BF),
            shape((rows * piece, WIDE), BF),
        ),
        in_specs=[ANY] * 7,
        out_specs=[VMEM] * 3,
        scratch_shapes=[
            pltpu.VMEM((32, depth), F32),
            pltpu.VMEM((heads * 32, WIDE), BF),
            pltpu.SMEM(fresh_slot.shape, jnp.int32),
            pltpu.SMEM(lengths.shape, jnp.int32),
            pltpu.SMEM(positions.shape, jnp.int32),
            pltpu.VMEM(query_latent.shape, BF),
            pltpu.VMEM((chunks, depth // chunks, heads * HEAD), BF),
            pltpu.VMEM((heads, NOPE, LAT), BF),
            pltpu.VMEM(freqs.shape, F32),
            pltpu.SemaphoreType.DMA((chunks + 6,)),
        ],
        compiler_params=params(16),
        name="project",
    )(*map(in_hbm, (fresh_slot, lengths, positions, query_latent, w_query, w_key_up, freqs)))

    own_out, own_stat, order = pl.pallas_call(
        functools.partial(own_keys_kernel, slots),
        out_shape=(
            shape((rows * piece, LAT), F32),
            shape((rows * piece, 256), F32),
            shape((32, rows * piece), BF),
        ),
        in_specs=[SMEM] * 2 + [VMEM] * 3,
        out_specs=[VMEM] * 3,
        scratch_shapes=[pltpu.VMEM((32, LAT + ROPE), F32)],
        compiler_params=params(32),
        name="own_keys",
    )(fresh_slot, positions, new_latent, freqs, own_q)

    def exchange(x, axes, n):
        return lax.all_to_all(x.reshape(n, -1, WIDE), axes, 0, 0, tiled=True).reshape(-1, WIDE)

    def swap(x):
        return lax.ppermute(x, "core", [(0, 1), (1, 0)])

    def turned(x, k, sign):
        pairs = []
        for i in range(copies):
            pairs += [(2 * i, 2 * ((i + sign * k) % copies)), (2 * i + 1, 2 * ((i - sign * k) % copies) + 1)]
        return lax.ppermute(x, ("zx", "core"), pairs)

    new_own = exchange(out_q, ("group", "zx"), slots * copies)
    res_sib = swap(res_q)
    res_both = jnp.concatenate([res_q, res_sib], 0)
    near = [turned(res_both, k, 1) for k in range(1, copies // 2)]
    across = turned(res_q, copies // 2, 1)
    new_own, across, *near = lax.optimization_barrier((new_own, across, *near))
    new_other, across_sib, *far = map(swap, (new_own, across, *near))

    send, keep, stat = pl.pallas_call(
        functools.partial(attend_kernel, piece),
        out_shape=(shape((rows * half, WIDE), BF), shape((rows * half, LAT), F32), shape((rows * half, 128), BF)),
        in_specs=[ANY] + [VMEM] * (5 + copies),
        out_specs=[VMEM] * 3,
        scratch_shapes=[pltpu.VMEM((slots, LAT + ROPE, tokens), BF), pltpu.SemaphoreType.DMA((slots,))],
        compiler_params=params(24),
        cost_estimate=cost(rows * 5 * 10**8, rows * 2 * 10**6),
        name="attend",
    )(in_hbm(fresh), pltpu.with_memory_space_constraint(cache, pltpu.VMEM), new_own, new_other, *far, res_sib, across_sib, *near, res_q, across)

    new_part, *res_parts = pl.pallas_call(
        functools.partial(join_kernel, slots, piece),
        out_shape=(shape((slots * half, WIDE), BF),)
        + (shape((2 * resident * piece, WIDE), BF),) * len(near)
        + (shape((resident * piece, WIDE), BF),) * 2,
        in_specs=[VMEM] * 3,
        out_specs=(ANY,) + (VMEM,) * (len(near) + 2),
        scratch_shapes=[pltpu.VMEM((slots * half, WIDE), BF), pltpu.SemaphoreType.DMA((4,))],
        compiler_params=params(32),
        name="join_cores",
    )(swap(send), keep, stat)
    new_back = exchange(new_part, ("group", "zx"), slots * copies)
    *near, res_here, across = res_parts
    near = [turned(x, k + 1, -1) for k, x in enumerate(near)]
    across = turned(across, copies // 2, -1)
    own_out, own_stat, order, across, *near = lax.optimization_barrier((own_out, own_stat, order, across, *near))
    far = swap(jnp.concatenate([x[resident * piece :] for x in near], 0))
    res_back = [res_here, across, *near, far]

    return pl.pallas_call(
        functools.partial(finish_kernel, slots),
        out_shape=shape((rows, 2, heads * 128), BF),
        in_specs=[VMEM] * (5 + len(res_back)),
        out_specs=VMEM,
        compiler_params=params(32),
        name="finish",
    )(order, new_back, own_out, own_stat, w_value_up, *res_back)


def solution(mesh):
    groups, shards = mesh.devices.shape
    split = Mesh(mesh.devices.reshape(groups, shards // 2, 2), ("group", "zx", "core"))
    ctx = ("zx", "core")
    placed = (
        P("group", None, None),
        P(None, ctx),
        P(ctx, None, None),
        P(ctx, None, None),
        P("group", ctx, None),
        P("group", None, ctx, None),
        P("group", None, None),
        P("group"),
        P("group", None),
        P("group", None),
    )
    return jax.shard_map(
        local, mesh=split, in_specs=placed, out_specs=P("group", None, ctx), check_vma=False
    )
```

```python
import functools
import math

import jax
import jax.numpy as jnp
import numpy as np
from jax import lax
from jax.experimental import pallas as pl
from jax.experimental.pallas import tpu as pltpu
from jax.sharding import Mesh
from jax.sharding import PartitionSpec as P

LAT = 512
ROPE = 64
NOPE = 128
HEAD = NOPE + ROPE
WIDE = 640
SCALE = HEAD ** (-0.5)
NONE = -1e30
BF = jnp.bfloat16
F32 = jnp.float32

HALF_PI = (1.5703125, 0.0004825592041015625, 1.2676710047e-06)


def dot(a, b, contract=((1,), (0,))):
    return lax.dot_general(a, b, (contract, ((), ())), preferred_element_type=F32)


def iota(shape, dim):
    return lax.broadcasted_iota(jnp.int32, shape, dim)


def cos_sin(angle):
    turns = jnp.floor(angle * (2.0 / math.pi) + 0.5)
    rest = angle - turns * HALF_PI[0]
    rest = rest - turns * HALF_PI[1]
    rest = rest - turns * HALF_PI[2]
    sq = rest * rest
    sine = rest + rest * sq * (
        -1.6666654611e-1 + sq * (8.3321608736e-3 + sq * -1.9515295891e-4)
    )
    cosine = 1.0 - 0.5 * sq + sq * sq * (
        4.166664568298827e-2 + sq * (-1.388731625493765e-3 + sq * 2.443315711809948e-5)
    )
    quarter = turns.astype(jnp.int32) & 3
    swapped = (quarter & 1) == 1
    first = jnp.where(swapped, sine, cosine)
    second = jnp.where(swapped, cosine, sine)
    first = jnp.where((quarter == 1) | (quarter == 2), -first, first)
    second = jnp.where(quarter >= 2, -second, second)
    return first, second


def rope(values, cosine, signed_sine):
    half = ROPE // 2
    swapped = jnp.concatenate([values[:, half:], values[:, :half]], 1)
    return values * cosine + swapped * signed_sine


def per_row(get, rows, width):
    at = iota((32, 1), 0)
    out = jnp.zeros((32, 1), jnp.int32)
    for r in range(rows):
        for s in range(width):
            out = jnp.where(at // (2 // width) == r * width + s, get(r, s), out)
    return out


def angles_of(pos_ref, freq_ref, rows):
    at = per_row(lambda r, s: pos_ref[s, r], rows, 2).astype(F32)
    cosine, sine = cos_sin(at * freq_ref[...])
    signed = jnp.where(iota((1, ROPE), 1) < ROPE // 2, -1.0, 1.0) * sine
    return cosine, signed


def row_of(slot_ref, slots, resident, shape, dim, per):
    at = iota(shape, dim)
    slot = at // per
    out = slot - slots
    for j in range(slots):
        out = jnp.where(slot == slot_ref[0, j], resident + j, out)
    return out


def project_kernel(heads, slots, copies, slot_hbm, len_hbm, pos_hbm, ql_hbm, wq_hbm, wk_hbm, freq_hbm,
                   out_ref, res_ref, own_ref, rows_ref, all_ref, slot_ref, len_ref, pos_ref, ql_ref, wq_ref, wk_ref,
                   freq_ref, sems):
    rows = ql_ref.shape[0]
    resident = rows - slots
    chunks = wq_ref.shape[0]
    step = wq_ref.shape[1]
    small = ((ql_hbm, ql_ref), (slot_hbm, slot_ref), (len_hbm, len_ref), (pos_hbm, pos_ref), (freq_hbm, freq_ref))
    small = [pltpu.make_async_copy(*pair, sems.at[chunks + 1 + n]) for n, pair in enumerate(small)]
    loads = [
        pltpu.make_async_copy(wq_hbm.at[pl.ds(c * step, step)], wq_ref.at[c], sems.at[c]) for c in range(chunks)
    ]
    loads.append(pltpu.make_async_copy(wk_hbm, wk_ref, sems.at[chunks]))
    for load in small + loads:
        load.start()
    for load in small:
        load.wait()
    rows_ref[...] = jnp.zeros_like(rows_ref)
    for r in range(rows):
        rows_ref[2 * r : 2 * r + 2, :] = ql_ref[r].astype(F32)
    cosine, signed = angles_of(pos_ref, freq_ref, rows)
    length = per_row(lambda r, s: len_ref[r], rows, 1)
    lane = iota((1, WIDE - LAT - ROPE), 1)
    meta = jnp.where(lane == 0, (length // 128).astype(F32), jnp.where(lane == 1, (length % 128).astype(F32), 0.0))
    piece = 2 * heads
    count = rows * piece
    row = row_of(slot_ref, slots, resident, (count, 1), 0, piece)
    inner = iota((count, 1), 0) % piece
    source = (inner // 2) * 32 + 2 * row + inner % 2
    select = jnp.where(iota((count, heads * 32), 1) == source, 1.0, 0.0).astype(BF)
    qfull = 0.0
    for c in range(chunks):
        loads[c].wait()
        qfull = qfull + dot(rows_ref[:, c * step : (c + 1) * step].astype(BF), wq_ref[c])
    qfull = qfull.astype(BF)
    loads[chunks].wait()
    for h in range(heads):
        part = qfull[:, h * HEAD : (h + 1) * HEAD]
        all_ref[h * 32 : (h + 1) * 32, :LAT] = dot(part[:, :NOPE], wk_ref[h]).astype(BF)
        tail = jnp.concatenate([rope(part[:, NOPE:].astype(F32), cosine, signed), meta], 1)
        all_ref[h * 32 : (h + 1) * 32, LAT:] = tail.astype(BF)
    own = dot(select, all_ref[...])
    own_ref[...] = own.astype(BF)
    for p in range(slots):
        one = own[p * piece : (p + 1) * piece]
        two = jnp.concatenate([one, one], 0).astype(BF)
        for k in range(0, copies, 2):
            at = (p * copies + k) * piece
            out_ref[at : at + 2 * piece, :] = two
    res_ref[...] = own[slots * piece :].astype(BF)


def own_keys_kernel(slots, slot_ref, pos_ref, nl_ref, freq_ref, own_ref, out_ref, stat_ref, order_ref, keys_ref):
    rows = nl_ref.shape[0]
    resident = rows - slots
    count = own_ref.shape[0]
    piece = count // rows
    keys_ref[...] = jnp.zeros_like(keys_ref)
    for r in range(rows):
        keys_ref[2 * r : 2 * r + 2, :] = nl_ref[r].astype(F32)
    cosine, signed = angles_of(pos_ref, freq_ref, rows)
    latent = keys_ref[:, :LAT].astype(BF)
    turned = rope(keys_ref[:, LAT:], cosine, signed).astype(BF)
    scores = dot(own_ref[:, :LAT], latent, ((1,), (1,)))
    scores = scores + dot(own_ref[:, LAT : LAT + ROPE], turned, ((1,), (1,)))
    scores = scores * SCALE
    row = row_of(slot_ref, slots, resident, (count, 1), 0, piece)
    step = iota((count, 1), 0) % 2
    key = iota((1, 32), 1)
    allowed = (key // 2 == row) & (key % 2 <= step)
    highest = jnp.max(jnp.where(allowed, scores, NONE), 1, keepdims=True)
    weights = jnp.where(allowed, jnp.exp(scores - highest), 0.0)
    total = jnp.sum(weights, 1, keepdims=True)
    out_ref[...] = dot(weights.astype(BF), latent)
    stat_ref[:, :128] = jnp.broadcast_to(highest, (count, 128))
    stat_ref[:, 128:] = jnp.broadcast_to(total, (count, 128))
    row = row_of(slot_ref, slots, resident, (1, count), 1, piece)
    target = 2 * row + iota((1, count), 1) % 2
    order_ref[...] = jnp.where(iota((32, count), 0) == target, 1.0, 0.0).astype(BF)


def parts_of(value):
    first = value.astype(BF).astype(F32)
    second = (value - first).astype(BF).astype(F32)
    return first, second, value - first - second


def with_stats(highest, total):
    lane = iota((1, 128), 1)
    out = 0.0
    for at, part in enumerate(parts_of(highest) + parts_of(total)):
        out = jnp.where(lane == at, part, out)
    return out.astype(BF)


def stats_of(tail):
    at = iota((128, 256), 0)
    pick = jnp.where((at < 6) & (at // 3 == iota((128, 256), 1) // 128), 1.0, 0.0).astype(BF)
    both = dot(tail, pick)
    return both[:, :128], both[:, 128:]


def spread(value):
    return jnp.concatenate([value] * (LAT // 128), -1)


def softmax_part(scores, length):
    scores = jnp.where(iota((1, scores.shape[1]), 1) < length, scores, NONE)
    highest = jnp.max(scores, 1, keepdims=True)
    weights = jnp.exp((scores - jnp.maximum(highest, 0.1 * NONE)) * SCALE)
    return highest * SCALE, jnp.sum(weights, 1, keepdims=True), weights.astype(BF)


def attend_kernel(piece, fresh_hbm, cache_ref, new_own, new_other, *refs):
    send_ref, keep_ref, stat_ref, keys_ref, sems = refs[-5:]
    blocks = refs[:-5]
    res_other, res_own = blocks[: len(blocks) // 2], blocks[len(blocks) // 2 :]
    slots, resident = fresh_hbm.shape[0], cache_ref.shape[0]
    rows = slots + resident
    half = new_own.shape[0] // slots
    loads = [pltpu.make_async_copy(fresh_hbm.at[i], keys_ref.at[i], sems.at[i]) for i in range(slots)]
    for load in loads:
        load.start()
    offset = (lax.axis_index("zx") * lax.axis_size("core") + lax.axis_index("core")) * keys_ref.shape[2]

    def queries_of(i):
        if i < slots:
            span = slice(i * half, (i + 1) * half)
            return jnp.concatenate([new_other[span, :], new_own[span, :]], 0)
        at = (i - slots) * piece
        step = resident * piece
        return jnp.concatenate(
            [ref[k + at : k + at + piece, :] for ref in res_other + res_own for k in range(0, ref.shape[0], step)], 0
        )

    def keys_of(i):
        return keys_ref.at[i] if i < slots else cache_ref.at[i - slots]

    def scores_of(i):
        queries = queries_of(i)
        length = queries[:, LAT + ROPE : LAT + ROPE + 2].astype(F32)
        length = (length[:, 0:1] * 128.0 + length[:, 1:2]).astype(jnp.int32) - offset
        return dot(queries[:, : LAT + ROPE], keys_of(i)[...]), length

    order = [*range(slots, rows), *range(slots)]
    arrived = 0
    ahead = scores_of(order[0])
    for n, i in enumerate(order):
        scores, length = ahead
        if n + 1 < rows:
            if order[n + 1] == arrived:
                upto = min(slots, arrived + n + 1)
                for load in loads[arrived:upto]:
                    load.wait()
                arrived = upto
            ahead = scores_of(order[n + 1])
        highest, total, weights = softmax_part(scores, length)
        mean = dot(weights, keys_of(i)[:LAT, :], ((1,), (1,))) * (1.0 / jnp.maximum(total, 1e-30))
        stats = with_stats(highest, total)
        span = slice(i * half, (i + 1) * half)
        send_ref[span, :LAT] = mean[:half].astype(BF)
        send_ref[span, LAT:] = stats[:half]
        keep_ref[span, :] = mean[half:]
        stat_ref[span, :] = stats[half:]


def joined(got, keep, stat):
    far_highest, far_total = stats_of(got[:, LAT:])
    highest, total = stats_of(stat)
    top = jnp.maximum(far_highest, highest)
    far_total = far_total * jnp.exp(far_highest - top)
    total = total * jnp.exp(highest - top)
    both = total + far_total
    scale = 1.0 / jnp.maximum(both, 1e-30)
    mean = got[:, :LAT].astype(F32) * spread(far_total * scale) + keep * spread(total * scale)
    return mean.astype(BF), with_stats(top, both)


def join_kernel(slots, piece, got_ref, keep_ref, stat_ref, new_hbm, *refs):
    res_refs, new_ref, sems = refs[:-2], refs[-2], refs[-1]
    count = new_ref.shape[0]
    half = count // slots
    resident = got_ref.shape[0] // half - slots
    parts = sems.shape[0]
    stores = []
    for c in range(parts):
        span = slice(c * count // parts, (c + 1) * count // parts)
        mean, stats = joined(got_ref[span, :], keep_ref[span, :], stat_ref[span, :])
        new_ref[span, :LAT] = mean
        new_ref[span, LAT:] = stats
        at = pl.ds(c * count // parts, count // parts)
        stores.append(pltpu.make_async_copy(new_ref.at[at], new_hbm.at[at], sems.at[c]))
        stores[c].start()
    mean, stats = joined(got_ref[count:, :], keep_ref[count:, :], stat_ref[count:, :])
    block = 0
    for ref in res_refs:
        for k in range(0, ref.shape[0], resident * piece):
            for i in range(resident):
                at = i * half + block * piece
                span = slice(k + i * piece, k + (i + 1) * piece)
                ref[span, :LAT] = mean[at : at + piece]
                ref[span, LAT:] = stats[at : at + piece]
            block += 1
    for store in stores:
        store.wait()


def merged(means, tails, own, own_highest, own_total):
    copies, n = means.shape[:2]
    highest, total = (x.reshape(copies, n, 128) for x in stats_of(tails.reshape(copies * n, 128)))
    top = jnp.maximum(jnp.max(highest, 0), own_highest)
    share = total * jnp.exp(highest - top[None])
    own_fade = jnp.exp(own_highest - top)
    scale = 1.0 / (jnp.sum(share, 0) + own_total * own_fade)
    summed = own * spread(own_fade * scale)
    share = share * scale[None]
    for k in range(copies):
        summed = summed + means[k].astype(F32) * spread(share[k])
    return summed.astype(BF)


def raised(latent, wv_ref, order):
    heads = wv_ref.shape[0]
    head = iota((latent.shape[0], 1), 0) % (2 * heads) // 2
    values = [jnp.where(head == h, dot(latent, wv_ref[h]), 0.0).astype(BF) for h in range(heads)]
    return dot(order, jnp.concatenate(values, 1))


def finish_new_kernel(slots, order_ref, new_ref, own_ref, stat_ref, wv_ref, out_ref):
    piece = 2 * wv_ref.shape[0]
    half = new_ref.shape[0] // slots
    latent = []
    for p in range(slots):
        block = new_ref[p * half : (p + 1) * half, :].reshape(half // piece, piece, WIDE)
        span = slice(p * piece, (p + 1) * piece)
        own = own_ref[span, :], stat_ref[span, :128], stat_ref[span, 128:]
        latent.append(merged(block[..., :LAT], block[..., LAT:], *own))
    out_ref[...] = raised(jnp.concatenate(latent, 0), wv_ref, order_ref[:, : slots * piece])


def finish_resident_kernel(slots, order_ref, own_ref, stat_ref, wv_ref, new_ref, *refs):
    *near_refs, far_ref, out_ref = refs
    rows = out_ref.shape[0]
    piece = 2 * wv_ref.shape[0]
    n = (rows - slots) * piece
    parts = [ref[:n, :] for ref in near_refs] + [far_ref[k : k + n, :] for k in range(0, far_ref.shape[0], n)]
    block = jnp.stack(parts)
    span = slice(slots * piece, rows * piece)
    own = own_ref[span, :], stat_ref[span, :128], stat_ref[span, 128:]
    latent = merged(block[..., :LAT], block[..., LAT:], *own)
    out = new_ref[...] + raised(latent, wv_ref, order_ref[:, slots * piece :])
    for r in range(rows):
        out_ref[r] = out[2 * r : 2 * r + 2].astype(BF)


VMEM = pl.BlockSpec(memory_space=pltpu.VMEM)
SMEM = pl.BlockSpec(memory_space=pltpu.SMEM)
ANY = pl.BlockSpec(memory_space=pl.ANY)


def shape(dims, dtype):
    return jax.ShapeDtypeStruct(dims, dtype)


def params(mebibytes):
    return pltpu.CompilerParams(vmem_limit_bytes=mebibytes * 1024 * 1024)


def cost(flops, moved):
    return pl.CostEstimate(flops=flops, bytes_accessed=moved, transcendentals=0)


def local(query_latent, w_query, w_key_up, w_value_up, cache, fresh, new_latent, lengths, fresh_slot, positions):
    rows, _, depth = query_latent.shape
    heads = w_key_up.shape[0]
    slots = fresh_slot.shape[1]
    resident = rows - slots
    tokens = cache.shape[1]
    copies = lax.axis_size("zx")
    piece = 2 * heads
    half = copies * piece
    chunks = 6
    freqs = 50000.0 ** (-np.arange(ROPE // 2, dtype=np.float64) / (ROPE // 2))
    freqs = jnp.asarray(np.concatenate([freqs, freqs]).astype(np.float32)[None])
    positions = positions.T
    cache = jnp.swapaxes(cache, 1, 2)
    fresh = jnp.swapaxes(fresh[0], 1, 2)

    def in_hbm(x):
        return pltpu.with_memory_space_constraint(x, pltpu.HBM)

    out_q, res_q, own_q = pl.pallas_call(
        functools.partial(project_kernel, heads, slots, copies),
        out_shape=(
            shape((slots * half, WIDE), BF),
            shape((resident * piece, WIDE), BF),
            shape((rows * piece, WIDE), BF),
        ),
        in_specs=[ANY] * 7,
        out_specs=[VMEM] * 3,
        scratch_shapes=[
            pltpu.VMEM((32, depth), F32),
            pltpu.VMEM((heads * 32, WIDE), BF),
            pltpu.SMEM(fresh_slot.shape, jnp.int32),
            pltpu.SMEM(lengths.shape, jnp.int32),
            pltpu.SMEM(positions.shape, jnp.int32),
            pltpu.VMEM(query_latent.shape, BF),
            pltpu.VMEM((chunks, depth // chunks, heads * HEAD), BF),
            pltpu.VMEM((heads, NOPE, LAT), BF),
            pltpu.VMEM(freqs.shape, F32),
            pltpu.SemaphoreType.DMA((chunks + 6,)),
        ],
        compiler_params=params(16),
        name="project",
    )(*map(in_hbm, (fresh_slot, lengths, positions, query_latent, w_query, w_key_up, freqs)))

    own_out, own_stat, order = pl.pallas_call(
        functools.partial(own_keys_kernel, slots),
        out_shape=(
            shape((rows * piece, LAT), F32),
            shape((rows * piece, 256), F32),
            shape((32, rows * piece), BF),
        ),
        in_specs=[SMEM] * 2 + [VMEM] * 3,
        out_specs=[VMEM] * 3,
        scratch_shapes=[pltpu.VMEM((32, LAT + ROPE), F32)],
        compiler_params=params(32),
        name="own_keys",
    )(fresh_slot, positions, new_latent, freqs, own_q)

    def exchange(x, axes, n):
        return lax.all_to_all(x.reshape(n, -1, WIDE), axes, 0, 0, tiled=True).reshape(-1, WIDE)

    def swap(x):
        return lax.ppermute(x, "core", [(0, 1), (1, 0)])

    def turned(x, k, sign):
        pairs = []
        for i in range(copies):
            pairs += [(2 * i, 2 * ((i + sign * k) % copies)), (2 * i + 1, 2 * ((i - sign * k) % copies) + 1)]
        return lax.ppermute(x, ("zx", "core"), pairs)

    new_own = exchange(out_q, ("group", "zx"), slots * copies)
    res_sib = swap(res_q)
    res_both = jnp.concatenate([res_q, res_sib], 0)
    near = [turned(res_both, k, 1) for k in range(1, copies // 2)]
    across = turned(res_q, copies // 2, 1)
    new_own, across, *near = lax.optimization_barrier((new_own, across, *near))
    new_other, across_sib, *far = map(swap, (new_own, across, *near))

    send, keep, stat = pl.pallas_call(
        functools.partial(attend_kernel, piece),
        out_shape=(shape((rows * half, WIDE), BF), shape((rows * half, LAT), F32), shape((rows * half, 128), BF)),
        in_specs=[ANY] + [VMEM] * (5 + copies),
        out_specs=[VMEM] * 3,
        scratch_shapes=[pltpu.VMEM((slots, LAT + ROPE, tokens), BF), pltpu.SemaphoreType.DMA((slots,))],
        compiler_params=params(24),
        cost_estimate=cost(rows * 5 * 10**8, rows * 2 * 10**6),
        name="attend",
    )(in_hbm(fresh), pltpu.with_memory_space_constraint(cache, pltpu.VMEM), new_own, new_other, *far, res_sib, across_sib, *near, res_q, across)

    new_part, *res_parts = pl.pallas_call(
        functools.partial(join_kernel, slots, piece),
        out_shape=(shape((slots * half, WIDE), BF),)
        + (shape((2 * resident * piece, WIDE), BF),) * len(near)
        + (shape((resident * piece, WIDE), BF),) * 2,
        in_specs=[VMEM] * 3,
        out_specs=(ANY,) + (VMEM,) * (len(near) + 2),
        scratch_shapes=[pltpu.VMEM((slots * half, WIDE), BF), pltpu.SemaphoreType.DMA((4,))],
        compiler_params=params(32),
        name="join_cores",
    )(swap(send), keep, stat)
    new_back = exchange(new_part, ("group", "zx"), slots * copies)
    *near, res_here, across = res_parts
    near = [turned(x, k + 1, -1) for k, x in enumerate(near)]
    across = turned(across, copies // 2, -1)
    own_out, own_stat, order, across, *near = lax.optimization_barrier((own_out, own_stat, order, across, *near))
    far = swap(jnp.concatenate([x[resident * piece :] for x in near], 0))
    res_back = [res_here, across, *near, far]

    new_out = pl.pallas_call(
        functools.partial(finish_new_kernel, slots),
        out_shape=shape((32, heads * 128), F32),
        in_specs=[VMEM] * 5,
        out_specs=VMEM,
        compiler_params=params(32),
        cost_estimate=cost(4 * 10**8, 2 * 10**6),
        name="finish_new",
    )(order, new_back, own_out, own_stat, w_value_up)

    return pl.pallas_call(
        functools.partial(finish_resident_kernel, slots),
        out_shape=shape((rows, 2, heads * 128), BF),
        in_specs=[VMEM] * (5 + len(res_back)),
        out_specs=VMEM,
        compiler_params=params(32),
        name="finish",
    )(order, own_out, own_stat, w_value_up, new_out, *res_back)


def solution(mesh):
    groups, shards = mesh.devices.shape
    split = Mesh(mesh.devices.reshape(groups, shards // 2, 2), ("group", "zx", "core"))
    ctx = ("zx", "core")
    placed = (
        P("group", None, None),
        P(None, ctx),
        P(ctx, None, None),
        P(ctx, None, None),
        P("group", ctx, None),
        P("group", None, ctx, None),
        P("group", None, None),
        P("group"),
        P("group", None),
        P("group", None),
    )
    return jax.shard_map(
        local, mesh=split, in_specs=placed, out_specs=P("group", None, ctx), check_vma=False
    )
```

```python
import functools
import math

import jax
import jax.numpy as jnp
import numpy as np
from jax import lax
from jax.experimental import pallas as pl
from jax.experimental.pallas import tpu as pltpu
from jax.sharding import Mesh
from jax.sharding import PartitionSpec as P

LAT = 512
ROPE = 64
NOPE = 128
HEAD = NOPE + ROPE
WIDE = 640
SCALE = HEAD ** (-0.5)
NONE = -1e30
BF = jnp.bfloat16
F32 = jnp.float32

HALF_PI = (1.5703125, 0.0004825592041015625, 1.2676710047e-06)


def dot(a, b, contract=((1,), (0,))):
    return lax.dot_general(a, b, (contract, ((), ())), preferred_element_type=F32)


def iota(shape, dim):
    return lax.broadcasted_iota(jnp.int32, shape, dim)


def cos_sin(angle):
    turns = jnp.floor(angle * (2.0 / math.pi) + 0.5)
    rest = angle - turns * HALF_PI[0]
    rest = rest - turns * HALF_PI[1]
    rest = rest - turns * HALF_PI[2]
    sq = rest * rest
    sine = rest + rest * sq * (
        -1.6666654611e-1 + sq * (8.3321608736e-3 + sq * -1.9515295891e-4)
    )
    cosine = 1.0 - 0.5 * sq + sq * sq * (
        4.166664568298827e-2 + sq * (-1.388731625493765e-3 + sq * 2.443315711809948e-5)
    )
    quarter = turns.astype(jnp.int32) & 3
    swapped = (quarter & 1) == 1
    first = jnp.where(swapped, sine, cosine)
    second = jnp.where(swapped, cosine, sine)
    first = jnp.where((quarter == 1) | (quarter == 2), -first, first)
    second = jnp.where(quarter >= 2, -second, second)
    return first, second


def rope(values, cosine, signed_sine):
    half = ROPE // 2
    swapped = jnp.concatenate([values[:, half:], values[:, :half]], 1)
    return values * cosine + swapped * signed_sine


def per_row(get, rows, width):
    at = iota((32, 1), 0)
    out = jnp.zeros((32, 1), jnp.int32)
    for r in range(rows):
        for s in range(width):
            out = jnp.where(at // (2 // width) == r * width + s, get(r, s), out)
    return out


def angles_of(pos_ref, freq_ref, rows):
    at = per_row(lambda r, s: pos_ref[s, r], rows, 2).astype(F32)
    cosine, sine = cos_sin(at * freq_ref[...])
    signed = jnp.where(iota((1, ROPE), 1) < ROPE // 2, -1.0, 1.0) * sine
    return cosine, signed


def row_of(slot_ref, slots, resident, shape, dim, per):
    at = iota(shape, dim)
    slot = at // per
    out = slot - slots
    for j in range(slots):
        out = jnp.where(slot == slot_ref[0, j], resident + j, out)
    return out


def project_kernel(heads, slots, copies, slot_hbm, len_hbm, pos_hbm, ql_hbm, wq_hbm, wk_hbm, freq_hbm,
                   out_ref, res_ref, own_ref, rows_ref, all_ref, slot_ref, len_ref, pos_ref, ql_ref, wq_ref, wk_ref,
                   freq_ref, sems):
    rows = ql_ref.shape[0]
    resident = rows - slots
    chunks = wq_ref.shape[0]
    step = wq_ref.shape[1]
    small = ((ql_hbm, ql_ref), (slot_hbm, slot_ref), (len_hbm, len_ref), (pos_hbm, pos_ref), (freq_hbm, freq_ref))
    small = [pltpu.make_async_copy(*pair, sems.at[chunks + 1 + n]) for n, pair in enumerate(small)]
    loads = [
        pltpu.make_async_copy(wq_hbm.at[pl.ds(c * step, step)], wq_ref.at[c], sems.at[c]) for c in range(chunks)
    ]
    loads.append(pltpu.make_async_copy(wk_hbm, wk_ref, sems.at[chunks]))
    for load in small + loads:
        load.start()
    for load in small:
        load.wait()
    rows_ref[...] = jnp.zeros_like(rows_ref)
    for r in range(rows):
        rows_ref[2 * r : 2 * r + 2, :] = ql_ref[r].astype(F32)
    cosine, signed = angles_of(pos_ref, freq_ref, rows)
    length = per_row(lambda r, s: len_ref[r], rows, 1)
    lane = iota((1, WIDE - LAT - ROPE), 1)
    meta = jnp.where(lane == 0, (length // 128).astype(F32), jnp.where(lane == 1, (length % 128).astype(F32), 0.0))
    piece = 2 * heads
    count = rows * piece
    row = row_of(slot_ref, slots, resident, (count, 1), 0, piece)
    inner = iota((count, 1), 0) % piece
    source = (inner // 2) * 32 + 2 * row + inner % 2
    select = jnp.where(iota((count, heads * 32), 1) == source, 1.0, 0.0).astype(BF)
    qfull = 0.0
    for c in range(chunks):
        loads[c].wait()
        qfull = qfull + dot(rows_ref[:, c * step : (c + 1) * step].astype(BF), wq_ref[c])
    qfull = qfull.astype(BF)
    loads[chunks].wait()
    for h in range(heads):
        part = qfull[:, h * HEAD : (h + 1) * HEAD]
        all_ref[h * 32 : (h + 1) * 32, :LAT] = dot(part[:, :NOPE], wk_ref[h]).astype(BF)
        tail = jnp.concatenate([rope(part[:, NOPE:].astype(F32), cosine, signed), meta], 1)
        all_ref[h * 32 : (h + 1) * 32, LAT:] = tail.astype(BF)
    own = dot(select, all_ref[...])
    own_ref[...] = own.astype(BF)
    for p in range(slots):
        one = own[p * piece : (p + 1) * piece]
        two = jnp.concatenate([one, one], 0).astype(BF)
        for k in range(0, copies, 2):
            at = (p * copies + k) * piece
            out_ref[at : at + 2 * piece, :] = two
    res_ref[...] = own[slots * piece :].astype(BF)


def own_keys_kernel(slots, slot_ref, pos_ref, nl_ref, freq_ref, own_ref, out_ref, stat_ref, order_ref, keys_ref):
    rows = nl_ref.shape[0]
    resident = rows - slots
    count = own_ref.shape[0]
    piece = count // rows
    keys_ref[...] = jnp.zeros_like(keys_ref)
    for r in range(rows):
        keys_ref[2 * r : 2 * r + 2, :] = nl_ref[r].astype(F32)
    cosine, signed = angles_of(pos_ref, freq_ref, rows)
    latent = keys_ref[:, :LAT].astype(BF)
    turned = rope(keys_ref[:, LAT:], cosine, signed).astype(BF)
    scores = dot(own_ref[:, :LAT], latent, ((1,), (1,)))
    scores = scores + dot(own_ref[:, LAT : LAT + ROPE], turned, ((1,), (1,)))
    scores = scores * SCALE
    row = row_of(slot_ref, slots, resident, (count, 1), 0, piece)
    step = iota((count, 1), 0) % 2
    key = iota((1, 32), 1)
    allowed = (key // 2 == row) & (key % 2 <= step)
    highest = jnp.max(jnp.where(allowed, scores, NONE), 1, keepdims=True)
    weights = jnp.where(allowed, jnp.exp(scores - highest), 0.0)
    total = jnp.sum(weights, 1, keepdims=True)
    out_ref[...] = dot(weights.astype(BF), latent)
    stat_ref[:, :128] = jnp.broadcast_to(highest, (count, 128))
    stat_ref[:, 128:] = jnp.broadcast_to(total, (count, 128))
    row = row_of(slot_ref, slots, resident, (1, count), 1, piece)
    target = 2 * row + iota((1, count), 1) % 2
    order_ref[...] = jnp.where(iota((32, count), 0) == target, 1.0, 0.0).astype(BF)


def parts_of(value):
    first = value.astype(BF).astype(F32)
    second = (value - first).astype(BF).astype(F32)
    return first, second, value - first - second


def with_stats(highest, total):
    lane = iota((1, 128), 1)
    out = 0.0
    for at, part in enumerate(parts_of(highest) + parts_of(total)):
        out = jnp.where(lane == at, part, out)
    return out.astype(BF)


def stats_of(tail):
    at = iota((128, 256), 0)
    pick = jnp.where((at < 6) & (at // 3 == iota((128, 256), 1) // 128), 1.0, 0.0).astype(BF)
    both = dot(tail, pick)
    return both[:, :128], both[:, 128:]


def spread(value):
    return jnp.concatenate([value] * (LAT // 128), -1)


def softmax_part(scores, length):
    scores = jnp.where(iota((1, scores.shape[1]), 1) < length, scores, NONE)
    highest = jnp.max(scores, 1, keepdims=True)
    weights = jnp.exp((scores - jnp.maximum(highest, 0.1 * NONE)) * SCALE)
    return highest * SCALE, jnp.sum(weights, 1, keepdims=True), weights.astype(BF)


def fetch_kernel(after_hbm, fresh_hbm, keys_ref, sem):
    load = pltpu.make_async_copy(fresh_hbm.at[pl.ds(0, keys_ref.shape[0])], keys_ref, sem)
    load.start()
    load.wait()


def attend_kernel(piece, fresh_hbm, first_ref, cache_ref, new_own, new_other, *refs):
    send_ref, keep_ref, stat_ref, keys_ref, sems = refs[-5:]
    blocks = refs[:-5]
    res_other, res_own = blocks[:2], blocks[2:]
    slots, resident = fresh_hbm.shape[0], cache_ref.shape[0]
    rows = slots + resident
    half = new_own.shape[0] // slots
    here = first_ref.shape[0]
    loads = [pltpu.make_async_copy(fresh_hbm.at[here + i], keys_ref.at[i], sems.at[i]) for i in range(slots - here)]
    for load in loads:
        load.start()
    offset = (lax.axis_index("zx") * lax.axis_size("core") + lax.axis_index("core")) * keys_ref.shape[2]

    def queries_of(i):
        if i < slots:
            span = slice(i * half, (i + 1) * half)
            return jnp.concatenate([new_other[span, :], new_own[span, :]], 0)
        at = (i - slots) * piece
        step = resident * piece
        return jnp.concatenate(
            [ref[k + at : k + at + piece, :] for ref in res_other + res_own for k in range(0, ref.shape[0], step)], 0
        )

    def keys_of(i):
        if i < here:
            return first_ref.at[i]
        return keys_ref.at[i - here] if i < slots else cache_ref.at[i - slots]

    def scores_of(i):
        queries = queries_of(i)
        length = queries[:, LAT + ROPE : LAT + ROPE + 2].astype(F32)
        length = (length[:, 0:1] * 128.0 + length[:, 1:2]).astype(jnp.int32) - offset
        return dot(queries[:, : LAT + ROPE], keys_of(i)[...]), length

    order = [*range(slots, rows), *range(slots)]
    arrived = here
    ahead = scores_of(order[0])
    for n, i in enumerate(order):
        scores, length = ahead
        if n + 1 < rows:
            if order[n + 1] == arrived:
                upto = min(slots, arrived + n + 1)
                for load in loads[arrived - here : upto - here]:
                    load.wait()
                arrived = upto
            ahead = scores_of(order[n + 1])
        highest, total, weights = softmax_part(scores, length)
        mean = dot(weights, keys_of(i)[:LAT, :], ((1,), (1,))) * (1.0 / jnp.maximum(total, 1e-30))
        stats = with_stats(highest, total)
        span = slice(i * half, (i + 1) * half)
        send_ref[span, :LAT] = mean[:half].astype(BF)
        send_ref[span, LAT:] = stats[:half]
        keep_ref[span, :] = mean[half:]
        stat_ref[span, :] = stats[half:]


def joined(got, keep, stat):
    far_highest, far_total = stats_of(got[:, LAT:])
    highest, total = stats_of(stat)
    top = jnp.maximum(far_highest, highest)
    far_total = far_total * jnp.exp(far_highest - top)
    total = total * jnp.exp(highest - top)
    both = total + far_total
    scale = 1.0 / jnp.maximum(both, 1e-30)
    mean = got[:, :LAT].astype(F32) * spread(far_total * scale) + keep * spread(total * scale)
    return mean.astype(BF), with_stats(top, both)


def join_kernel(slots, piece, got_ref, keep_ref, stat_ref, new_hbm, *refs):
    res_refs, new_ref, sems = refs[:-2], refs[-2], refs[-1]
    count = new_ref.shape[0]
    half = count // slots
    resident = got_ref.shape[0] // half - slots
    parts = sems.shape[0]
    stores = []
    for c in range(parts):
        span = slice(c * count // parts, (c + 1) * count // parts)
        mean, stats = joined(got_ref[span, :], keep_ref[span, :], stat_ref[span, :])
        new_ref[span, :LAT] = mean
        new_ref[span, LAT:] = stats
        at = pl.ds(c * count // parts, count // parts)
        stores.append(pltpu.make_async_copy(new_ref.at[at], new_hbm.at[at], sems.at[c]))
        stores[c].start()
    mean, stats = joined(got_ref[count:, :], keep_ref[count:, :], stat_ref[count:, :])
    block = 0
    for ref in res_refs:
        for k in range(0, ref.shape[0], resident * piece):
            for i in range(resident):
                at = i * half + block * piece
                span = slice(k + i * piece, k + (i + 1) * piece)
                ref[span, :LAT] = mean[at : at + piece]
                ref[span, LAT:] = stats[at : at + piece]
            block += 1
    for store in stores:
        store.wait()


def merged(means, tails, own, own_highest, own_total):
    copies, n = means.shape[:2]
    highest, total = (x.reshape(copies, n, 128) for x in stats_of(tails.reshape(copies * n, 128)))
    top = jnp.maximum(jnp.max(highest, 0), own_highest)
    share = total * jnp.exp(highest - top[None])
    own_fade = jnp.exp(own_highest - top)
    scale = 1.0 / (jnp.sum(share, 0) + own_total * own_fade)
    summed = own * spread(own_fade * scale)
    share = share * scale[None]
    for k in range(copies):
        summed = summed + means[k].astype(F32) * spread(share[k])
    return summed.astype(BF)


def raised(latent, wv_ref, order):
    heads = wv_ref.shape[0]
    head = iota((latent.shape[0], 1), 0) % (2 * heads) // 2
    values = [jnp.where(head == h, dot(latent, wv_ref[h]), 0.0).astype(BF) for h in range(heads)]
    return dot(order, jnp.concatenate(values, 1))


def finish_new_kernel(slots, order_ref, new_ref, own_ref, stat_ref, wv_ref, out_ref):
    piece = 2 * wv_ref.shape[0]
    half = new_ref.shape[0] // slots
    latent = []
    for p in range(slots):
        block = new_ref[p * half : (p + 1) * half, :].reshape(half // piece, piece, WIDE)
        span = slice(p * piece, (p + 1) * piece)
        own = own_ref[span, :], stat_ref[span, :128], stat_ref[span, 128:]
        latent.append(merged(block[..., :LAT], block[..., LAT:], *own))
    out_ref[...] = raised(jnp.concatenate(latent, 0), wv_ref, order_ref[:, : slots * piece])


def finish_resident_kernel(slots, order_ref, own_ref, stat_ref, wv_ref, new_ref, *refs):
    *near_refs, far_ref, out_ref = refs
    rows = out_ref.shape[0]
    piece = 2 * wv_ref.shape[0]
    n = (rows - slots) * piece
    parts = [ref[:n, :] for ref in near_refs] + [far_ref[k : k + n, :] for k in range(0, far_ref.shape[0], n)]
    block = jnp.stack(parts)
    span = slice(slots * piece, rows * piece)
    own = own_ref[span, :], stat_ref[span, :128], stat_ref[span, 128:]
    latent = merged(block[..., :LAT], block[..., LAT:], *own)
    out = new_ref[...] + raised(latent, wv_ref, order_ref[:, slots * piece :])
    for r in range(rows):
        out_ref[r] = out[2 * r : 2 * r + 2].astype(BF)


VMEM = pl.BlockSpec(memory_space=pltpu.VMEM)
SMEM = pl.BlockSpec(memory_space=pltpu.SMEM)
ANY = pl.BlockSpec(memory_space=pl.ANY)


def shape(dims, dtype):
    return jax.ShapeDtypeStruct(dims, dtype)


def params(mebibytes):
    return pltpu.CompilerParams(vmem_limit_bytes=mebibytes * 1024 * 1024)


def cost(flops, moved):
    return pl.CostEstimate(flops=flops, bytes_accessed=moved, transcendentals=0)


def local(query_latent, w_query, w_key_up, w_value_up, cache, fresh, new_latent, lengths, fresh_slot, positions):
    rows, _, depth = query_latent.shape
    heads = w_key_up.shape[0]
    slots = fresh_slot.shape[1]
    resident = rows - slots
    tokens = cache.shape[1]
    copies = lax.axis_size("zx")
    piece = 2 * heads
    half = copies * piece
    chunks = 6
    freqs = 50000.0 ** (-np.arange(ROPE // 2, dtype=np.float64) / (ROPE // 2))
    freqs = jnp.asarray(np.concatenate([freqs, freqs]).astype(np.float32)[None])
    positions = positions.T
    cache = jnp.swapaxes(cache, 1, 2)
    fresh = jnp.swapaxes(fresh[0], 1, 2)

    def in_vmem(x):
        return pltpu.with_memory_space_constraint(x, pltpu.VMEM)

    def in_hbm(x):
        return pltpu.with_memory_space_constraint(x, pltpu.HBM)

    out_q, res_q, own_q = pl.pallas_call(
        functools.partial(project_kernel, heads, slots, copies),
        out_shape=(
            shape((slots * half, WIDE), BF),
            shape((resident * piece, WIDE), BF),
            shape((rows * piece, WIDE), BF),
        ),
        in_specs=[ANY] * 7,
        out_specs=[VMEM] * 3,
        scratch_shapes=[
            pltpu.VMEM((32, depth), F32),
            pltpu.VMEM((heads * 32, WIDE), BF),
            pltpu.SMEM(fresh_slot.shape, jnp.int32),
            pltpu.SMEM(lengths.shape, jnp.int32),
            pltpu.SMEM(positions.shape, jnp.int32),
            pltpu.VMEM(query_latent.shape, BF),
            pltpu.VMEM((chunks, depth // chunks, heads * HEAD), BF),
            pltpu.VMEM((heads, NOPE, LAT), BF),
            pltpu.VMEM(freqs.shape, F32),
            pltpu.SemaphoreType.DMA((chunks + 6,)),
        ],
        compiler_params=params(16),
        name="project",
    )(*map(in_hbm, (fresh_slot, lengths, positions, query_latent, w_query, w_key_up, freqs)))

    own_out, own_stat, order = pl.pallas_call(
        functools.partial(own_keys_kernel, slots),
        out_shape=(
            shape((rows * piece, LAT), F32),
            shape((rows * piece, 256), F32),
            shape((32, rows * piece), BF),
        ),
        in_specs=[SMEM] * 2 + [VMEM] * 3,
        out_specs=[VMEM] * 3,
        scratch_shapes=[pltpu.VMEM((32, LAT + ROPE), F32)],
        compiler_params=params(32),
        name="own_keys",
    )(fresh_slot, positions, new_latent, freqs, own_q)

    def exchange(x, axes, n):
        return lax.all_to_all(x.reshape(n, -1, WIDE), axes, 0, 0, tiled=True).reshape(-1, WIDE)

    def swap(x):
        return lax.ppermute(x, "core", [(0, 1), (1, 0)])

    def turned(x, k, sign):
        pairs = []
        for i in range(copies):
            pairs += [(2 * i, 2 * ((i + sign * k) % copies)), (2 * i + 1, 2 * ((i - sign * k) % copies) + 1)]
        return lax.ppermute(x, ("zx", "core"), pairs)

    new_own = exchange(out_q, ("group", "zx"), slots * copies)
    res_sib = swap(res_q)
    res_both = jnp.concatenate([res_q, res_sib], 0)
    turns = sorted(range(1, copies // 2), key=lambda k: (k + 1) % 2 * copies - k)
    near = [turned(res_both, k, 1) for k in turns]
    across = turned(res_q, copies // 2, 1)
    new_own, across, *near = lax.optimization_barrier((new_own, across, *near))
    new_other = swap(new_own)
    far = swap(jnp.concatenate([*near, across], 0))
    first = 2
    first_keys = pl.pallas_call(
        fetch_kernel,
        out_shape=pltpu.VMEM((first, *fresh.shape[1:]), BF),
        in_specs=[ANY] * 2,
        out_specs=ANY,
        scratch_shapes=[pltpu.SemaphoreType.DMA],
        compiler_params=params(2),
        cost_estimate=cost(0, 4 * first * fresh[0].size),
        name="fetch_keys",
    )(new_own, in_hbm(fresh))

    send, keep, stat = pl.pallas_call(
        functools.partial(attend_kernel, piece),
        out_shape=(shape((rows * half, WIDE), BF), shape((rows * half, LAT), F32), shape((rows * half, 128), BF)),
        in_specs=[ANY] + [VMEM] * (8 + len(near)),
        out_specs=[VMEM] * 3,
        scratch_shapes=[
            pltpu.VMEM((slots - first, LAT + ROPE, tokens), BF),
            pltpu.SemaphoreType.DMA((slots - first,)),
        ],
        compiler_params=params(24),
        cost_estimate=cost(rows * 5 * 10**8, rows * 2 * 10**6),
        name="attend",
    )(in_hbm(fresh), in_vmem(first_keys), in_vmem(cache), new_own, new_other, far, res_sib, *near, across, res_q)

    new_part, *res_parts = pl.pallas_call(
        functools.partial(join_kernel, slots, piece),
        out_shape=(shape((slots * half, WIDE), BF),)
        + (shape((2 * resident * piece, WIDE), BF),) * len(near)
        + (shape((resident * piece, WIDE), BF),) * 2,
        in_specs=[VMEM] * 3,
        out_specs=(ANY,) + (VMEM,) * (len(near) + 2),
        scratch_shapes=[pltpu.VMEM((slots * half, WIDE), BF), pltpu.SemaphoreType.DMA((4,))],
        compiler_params=params(32),
        name="join_cores",
    )(swap(send), keep, stat)
    new_back = exchange(new_part, ("group", "zx"), slots * copies)
    *near, across, res_here = res_parts
    near = [turned(x, k, -1) for k, x in zip(turns, near)]
    across = turned(across, copies // 2, -1)
    own_out, own_stat, order, across, *near = lax.optimization_barrier((own_out, own_stat, order, across, *near))
    far = swap(jnp.concatenate([x[resident * piece :] for x in near], 0))
    res_back = [res_here, across, *near, far]

    new_out = pl.pallas_call(
        functools.partial(finish_new_kernel, slots),
        out_shape=shape((32, heads * 128), F32),
        in_specs=[VMEM] * 5,
        out_specs=VMEM,
        compiler_params=params(32),
        cost_estimate=cost(4 * 10**8, 2 * 10**6),
        name="finish_new",
    )(order, new_back, own_out, own_stat, w_value_up)

    return pl.pallas_call(
        functools.partial(finish_resident_kernel, slots),
        out_shape=shape((rows, 2, heads * 128), BF),
        in_specs=[VMEM] * (5 + len(res_back)),
        out_specs=VMEM,
        compiler_params=params(32),
        name="finish",
    )(order, own_out, own_stat, w_value_up, new_out, *res_back)


def solution(mesh):
    groups, shards = mesh.devices.shape
    split = Mesh(mesh.devices.reshape(groups, shards // 2, 2), ("group", "zx", "core"))
    ctx = ("zx", "core")
    placed = (
        P("group", None, None),
        P(None, ctx),
        P(ctx, None, None),
        P(ctx, None, None),
        P("group", ctx, None),
        P("group", None, ctx, None),
        P("group", None, None),
        P("group"),
        P("group", None),
        P("group", None),
    )
    return jax.shard_map(
        local, mesh=split, in_specs=placed, out_specs=P("group", None, ctx), check_vma=False
    )
```

```python
import functools
import math

import jax
import jax.numpy as jnp
import numpy as np
from jax import lax
from jax.experimental import pallas as pl
from jax.experimental.pallas import tpu as pltpu
from jax.sharding import Mesh
from jax.sharding import PartitionSpec as P

LAT = 512
ROPE = 64
NOPE = 128
HEAD = NOPE + ROPE
WIDE = 640
SCALE = HEAD ** (-0.5)
NONE = -1e30
BF = jnp.bfloat16
F32 = jnp.float32

HALF_PI = (1.5703125, 0.0004825592041015625, 1.2676710047e-06)


def dot(a, b, contract=((1,), (0,))):
    return lax.dot_general(a, b, (contract, ((), ())), preferred_element_type=F32)


def iota(shape, dim):
    return lax.broadcasted_iota(jnp.int32, shape, dim)


def cos_sin(angle):
    turns = jnp.floor(angle * (2.0 / math.pi) + 0.5)
    rest = angle - turns * HALF_PI[0]
    rest = rest - turns * HALF_PI[1]
    rest = rest - turns * HALF_PI[2]
    sq = rest * rest
    sine = rest + rest * sq * (
        -1.6666654611e-1 + sq * (8.3321608736e-3 + sq * -1.9515295891e-4)
    )
    cosine = 1.0 - 0.5 * sq + sq * sq * (
        4.166664568298827e-2 + sq * (-1.388731625493765e-3 + sq * 2.443315711809948e-5)
    )
    quarter = turns.astype(jnp.int32) & 3
    swapped = (quarter & 1) == 1
    first = jnp.where(swapped, sine, cosine)
    second = jnp.where(swapped, cosine, sine)
    first = jnp.where((quarter == 1) | (quarter == 2), -first, first)
    second = jnp.where(quarter >= 2, -second, second)
    return first, second


def rope(values, cosine, signed_sine):
    half = ROPE // 2
    swapped = jnp.concatenate([values[:, half:], values[:, :half]], 1)
    return values * cosine + swapped * signed_sine


def per_row(get, rows, width):
    at = iota((32, 1), 0)
    out = jnp.zeros((32, 1), jnp.int32)
    for r in range(rows):
        for s in range(width):
            out = jnp.where(at // (2 // width) == r * width + s, get(r, s), out)
    return out


def angles_of(pos_ref, freq_ref, rows):
    at = per_row(lambda r, s: pos_ref[s, r], rows, 2).astype(F32)
    cosine, sine = cos_sin(at * freq_ref[...])
    signed = jnp.where(iota((1, ROPE), 1) < ROPE // 2, -1.0, 1.0) * sine
    return cosine, signed


def row_of(slot_ref, slots, resident, shape, dim, per):
    at = iota(shape, dim)
    slot = at // per
    out = slot - slots
    for j in range(slots):
        out = jnp.where(slot == slot_ref[0, j], resident + j, out)
    return out


def project_kernel(heads, slots, copies, slot_hbm, len_hbm, pos_hbm, ql_hbm, wq_hbm, wk_hbm, freq_hbm,
                   out_ref, res_ref, own_ref, rows_ref, all_ref, slot_ref, len_ref, pos_ref, ql_ref, wq_ref, wk_ref,
                   freq_ref, sems):
    rows = ql_ref.shape[0]
    resident = rows - slots
    chunks = wq_ref.shape[0]
    step = wq_ref.shape[1]
    small = ((ql_hbm, ql_ref), (slot_hbm, slot_ref), (len_hbm, len_ref), (pos_hbm, pos_ref), (freq_hbm, freq_ref))
    small = [pltpu.make_async_copy(*pair, sems.at[chunks + 1 + n]) for n, pair in enumerate(small)]
    loads = [
        pltpu.make_async_copy(wq_hbm.at[pl.ds(c * step, step)], wq_ref.at[c], sems.at[c]) for c in range(chunks)
    ]
    loads.append(pltpu.make_async_copy(wk_hbm, wk_ref, sems.at[chunks]))
    for load in small + loads:
        load.start()
    for load in small:
        load.wait()
    rows_ref[...] = jnp.zeros_like(rows_ref)
    for r in range(rows):
        rows_ref[2 * r : 2 * r + 2, :] = ql_ref[r].astype(F32)
    cosine, signed = angles_of(pos_ref, freq_ref, rows)
    length = per_row(lambda r, s: len_ref[r], rows, 1)
    lane = iota((1, WIDE - LAT - ROPE), 1)
    meta = jnp.where(lane == 0, (length // 128).astype(F32), jnp.where(lane == 1, (length % 128).astype(F32), 0.0))
    piece = 2 * heads
    count = rows * piece
    row = row_of(slot_ref, slots, resident, (count, 1), 0, piece)
    inner = iota((count, 1), 0) % piece
    source = (inner // 2) * 32 + 2 * row + inner % 2
    select = jnp.where(iota((count, heads * 32), 1) == source, 1.0, 0.0).astype(BF)
    qfull = 0.0
    for c in range(chunks):
        loads[c].wait()
        qfull = qfull + dot(rows_ref[:, c * step : (c + 1) * step].astype(BF), wq_ref[c])
    qfull = qfull.astype(BF)
    loads[chunks].wait()
    for h in range(heads):
        part = qfull[:, h * HEAD : (h + 1) * HEAD]
        all_ref[h * 32 : (h + 1) * 32, :LAT] = dot(part[:, :NOPE], wk_ref[h]).astype(BF)
        tail = jnp.concatenate([rope(part[:, NOPE:].astype(F32), cosine, signed), meta], 1)
        all_ref[h * 32 : (h + 1) * 32, LAT:] = tail.astype(BF)
    own = dot(select, all_ref[...])
    own_ref[...] = own.astype(BF)
    for p in range(slots):
        one = own[p * piece : (p + 1) * piece]
        two = jnp.concatenate([one, one], 0).astype(BF)
        for k in range(0, copies, 2):
            at = (p * copies + k) * piece
            out_ref[at : at + 2 * piece, :] = two
    res_ref[...] = own[slots * piece :].astype(BF)


def own_keys_kernel(slots, slot_ref, pos_ref, nl_ref, freq_ref, own_ref, out_ref, stat_ref, order_ref, keys_ref):
    rows = nl_ref.shape[0]
    resident = rows - slots
    count = own_ref.shape[0]
    piece = count // rows
    keys_ref[...] = jnp.zeros_like(keys_ref)
    for r in range(rows):
        keys_ref[2 * r : 2 * r + 2, :] = nl_ref[r].astype(F32)
    cosine, signed = angles_of(pos_ref, freq_ref, rows)
    latent = keys_ref[:, :LAT].astype(BF)
    turned = rope(keys_ref[:, LAT:], cosine, signed).astype(BF)
    scores = dot(own_ref[:, :LAT], latent, ((1,), (1,)))
    scores = scores + dot(own_ref[:, LAT : LAT + ROPE], turned, ((1,), (1,)))
    scores = scores * SCALE
    row = row_of(slot_ref, slots, resident, (count, 1), 0, piece)
    step = iota((count, 1), 0) % 2
    key = iota((1, 32), 1)
    allowed = (key // 2 == row) & (key % 2 <= step)
    highest = jnp.max(jnp.where(allowed, scores, NONE), 1, keepdims=True)
    weights = jnp.where(allowed, jnp.exp(scores - highest), 0.0)
    total = jnp.sum(weights, 1, keepdims=True)
    out_ref[...] = dot(weights.astype(BF), latent)
    stat_ref[:, :128] = jnp.broadcast_to(highest, (count, 128))
    stat_ref[:, 128:] = jnp.broadcast_to(total, (count, 128))
    row = row_of(slot_ref, slots, resident, (1, count), 1, piece)
    target = 2 * row + iota((1, count), 1) % 2
    order_ref[...] = jnp.where(iota((32, count), 0) == target, 1.0, 0.0).astype(BF)


def parts_of(value):
    first = value.astype(BF).astype(F32)
    second = (value - first).astype(BF).astype(F32)
    return first, second, value - first - second


def with_stats(highest, total):
    lane = iota((1, 128), 1)
    out = 0.0
    for at, part in enumerate(parts_of(highest) + parts_of(total)):
        out = jnp.where(lane == at, part, out)
    return out.astype(BF)


def stats_of(tail):
    at = iota((128, 256), 0)
    pick = jnp.where((at < 6) & (at // 3 == iota((128, 256), 1) // 128), 1.0, 0.0).astype(BF)
    both = dot(tail, pick)
    return both[:, :128], both[:, 128:]


def spread(value):
    return jnp.concatenate([value] * (LAT // 128), -1)


def softmax_part(scores, length):
    scores = jnp.where(iota((1, scores.shape[1]), 1) < length, scores, NONE)
    highest = jnp.max(scores, 1, keepdims=True)
    weights = jnp.exp((scores - jnp.maximum(highest, 0.1 * NONE)) * SCALE)
    return highest * SCALE, jnp.sum(weights, 1, keepdims=True), weights.astype(BF)


def fetch_kernel(after_hbm, fresh_hbm, keys_ref, sem):
    load = pltpu.make_async_copy(fresh_hbm.at[pl.ds(0, keys_ref.shape[0])], keys_ref, sem)
    load.start()
    load.wait()


def attend_kernel(piece, fresh_hbm, first_ref, cache_ref, new_own, new_other, *refs):
    send_ref, keep_ref, stat_ref, keys_ref, sems = refs[-5:]
    blocks = refs[:-5]
    res_other, res_own = blocks[:2], blocks[2:]
    slots, resident = fresh_hbm.shape[0], cache_ref.shape[0]
    rows = slots + resident
    half = new_own.shape[0] // slots
    here = first_ref.shape[0]
    loads = [pltpu.make_async_copy(fresh_hbm.at[here + i], keys_ref.at[i], sems.at[i]) for i in range(slots - here)]
    for load in loads:
        load.start()
    offset = (lax.axis_index("zx") * lax.axis_size("core") + lax.axis_index("core")) * keys_ref.shape[2]

    def queries_of(i):
        if i < slots:
            span = slice(i * half, (i + 1) * half)
            return jnp.concatenate([new_other[span, :], new_own[span, :]], 0)
        at = (i - slots) * piece
        step = resident * piece
        return jnp.concatenate(
            [ref[k + at : k + at + piece, :] for ref in res_other + res_own for k in range(0, ref.shape[0], step)], 0
        )

    def keys_of(i):
        if i < here:
            return first_ref.at[i]
        return keys_ref.at[i - here] if i < slots else cache_ref.at[i - slots]

    def scores_of(i):
        queries = queries_of(i)
        length = queries[:, LAT + ROPE : LAT + ROPE + 2].astype(F32)
        length = (length[:, 0:1] * 128.0 + length[:, 1:2]).astype(jnp.int32) - offset
        return dot(queries[:, : LAT + ROPE], keys_of(i)[...]), length

    order = [*range(slots, rows), *range(slots)]
    arrived = here
    ahead = scores_of(order[0])
    for n, i in enumerate(order):
        scores, length = ahead
        if n + 1 < rows:
            if order[n + 1] == arrived:
                upto = min(slots, arrived + 3)
                for load in loads[arrived - here : upto - here]:
                    load.wait()
                arrived = upto
            ahead = scores_of(order[n + 1])
        highest, total, weights = softmax_part(scores, length)
        mean = dot(weights, keys_of(i)[:LAT, :], ((1,), (1,))) * (1.0 / jnp.maximum(total, 1e-30))
        stats = with_stats(highest, total)
        span = slice(i * half, (i + 1) * half)
        send_ref[span, :LAT] = mean[:half].astype(BF)
        send_ref[span, LAT:] = stats[:half]
        keep_ref[span, :] = mean[half:]
        stat_ref[span, :] = stats[half:]


def joined(got, keep, stat):
    far_highest, far_total = stats_of(got[:, LAT:])
    highest, total = stats_of(stat)
    top = jnp.maximum(far_highest, highest)
    far_total = far_total * jnp.exp(far_highest - top)
    total = total * jnp.exp(highest - top)
    both = total + far_total
    scale = 1.0 / jnp.maximum(both, 1e-30)
    mean = got[:, :LAT].astype(F32) * spread(far_total * scale) + keep * spread(total * scale)
    return mean.astype(BF), with_stats(top, both)


def join_kernel(slots, piece, got_ref, keep_ref, stat_ref, new_hbm, *refs):
    res_refs, new_ref, sems = refs[:-2], refs[-2], refs[-1]
    count = new_ref.shape[0]
    half = count // slots
    resident = got_ref.shape[0] // half - slots
    parts = sems.shape[0]
    stores = []
    for c in range(parts):
        span = slice(c * count // parts, (c + 1) * count // parts)
        mean, stats = joined(got_ref[span, :], keep_ref[span, :], stat_ref[span, :])
        new_ref[span, :LAT] = mean
        new_ref[span, LAT:] = stats
        at = pl.ds(c * count // parts, count // parts)
        stores.append(pltpu.make_async_copy(new_ref.at[at], new_hbm.at[at], sems.at[c]))
        stores[c].start()
    mean, stats = joined(got_ref[count:, :], keep_ref[count:, :], stat_ref[count:, :])
    block = 0
    for ref in res_refs:
        for k in range(0, ref.shape[0], resident * piece):
            for i in range(resident):
                at = i * half + block * piece
                span = slice(k + i * piece, k + (i + 1) * piece)
                ref[span, :LAT] = mean[at : at + piece]
                ref[span, LAT:] = stats[at : at + piece]
            block += 1
    for store in stores:
        store.wait()


def merged(means, tails, own, own_highest, own_total):
    copies, n = means.shape[:2]
    highest, total = (x.reshape(copies, n, 128) for x in stats_of(tails.reshape(copies * n, 128)))
    top = jnp.maximum(jnp.max(highest, 0), own_highest)
    share = total * jnp.exp(highest - top[None])
    own_fade = jnp.exp(own_highest - top)
    scale = 1.0 / (jnp.sum(share, 0) + own_total * own_fade)
    summed = own * spread(own_fade * scale)
    share = share * scale[None]
    for k in range(copies):
        summed = summed + means[k].astype(F32) * spread(share[k])
    return summed.astype(BF)


def raised(latent, wv_ref, order):
    heads = wv_ref.shape[0]
    head = iota((latent.shape[0], 1), 0) % (2 * heads) // 2
    values = [jnp.where(head == h, dot(latent, wv_ref[h]), 0.0).astype(BF) for h in range(heads)]
    return dot(order, jnp.concatenate(values, 1))


def finish_new_kernel(slots, order_ref, new_ref, own_ref, stat_ref, wv_ref, out_ref):
    piece = 2 * wv_ref.shape[0]
    half = new_ref.shape[0] // slots
    latent = []
    for p in range(slots):
        block = new_ref[p * half : (p + 1) * half, :].reshape(half // piece, piece, WIDE)
        span = slice(p * piece, (p + 1) * piece)
        own = own_ref[span, :], stat_ref[span, :128], stat_ref[span, 128:]
        latent.append(merged(block[..., :LAT], block[..., LAT:], *own))
    out_ref[...] = raised(jnp.concatenate(latent, 0), wv_ref, order_ref[:, : slots * piece])


def finish_resident_kernel(slots, order_ref, own_ref, stat_ref, wv_ref, new_ref, *refs):
    *near_refs, far_ref, out_ref = refs
    rows = out_ref.shape[0]
    piece = 2 * wv_ref.shape[0]
    n = (rows - slots) * piece
    parts = [ref[:n, :] for ref in near_refs] + [far_ref[k : k + n, :] for k in range(0, far_ref.shape[0], n)]
    block = jnp.stack(parts)
    span = slice(slots * piece, rows * piece)
    own = own_ref[span, :], stat_ref[span, :128], stat_ref[span, 128:]
    latent = merged(block[..., :LAT], block[..., LAT:], *own)
    out = new_ref[...] + raised(latent, wv_ref, order_ref[:, slots * piece :])
    for r in range(rows):
        out_ref[r] = out[2 * r : 2 * r + 2].astype(BF)


VMEM = pl.BlockSpec(memory_space=pltpu.VMEM)
SMEM = pl.BlockSpec(memory_space=pltpu.SMEM)
ANY = pl.BlockSpec(memory_space=pl.ANY)


def shape(dims, dtype):
    return jax.ShapeDtypeStruct(dims, dtype)


def params(mebibytes):
    return pltpu.CompilerParams(vmem_limit_bytes=mebibytes * 1024 * 1024)


def cost(flops, moved):
    return pl.CostEstimate(flops=flops, bytes_accessed=moved, transcendentals=0)


def local(query_latent, w_query, w_key_up, w_value_up, cache, fresh, new_latent, lengths, fresh_slot, positions):
    rows, _, depth = query_latent.shape
    heads = w_key_up.shape[0]
    slots = fresh_slot.shape[1]
    resident = rows - slots
    tokens = cache.shape[1]
    copies = lax.axis_size("zx")
    piece = 2 * heads
    half = copies * piece
    chunks = 6
    freqs = 50000.0 ** (-np.arange(ROPE // 2, dtype=np.float64) / (ROPE // 2))
    freqs = jnp.asarray(np.concatenate([freqs, freqs]).astype(np.float32)[None])
    positions = positions.T
    cache = jnp.swapaxes(cache, 1, 2)
    fresh = jnp.swapaxes(fresh[0], 1, 2)

    def in_vmem(x):
        return pltpu.with_memory_space_constraint(x, pltpu.VMEM)

    def in_hbm(x):
        return pltpu.with_memory_space_constraint(x, pltpu.HBM)

    out_q, res_q, own_q = pl.pallas_call(
        functools.partial(project_kernel, heads, slots, copies),
        out_shape=(
            shape((slots * half, WIDE), BF),
            shape((resident * piece, WIDE), BF),
            shape((rows * piece, WIDE), BF),
        ),
        in_specs=[ANY] * 7,
        out_specs=[VMEM] * 3,
        scratch_shapes=[
            pltpu.VMEM((32, depth), F32),
            pltpu.VMEM((heads * 32, WIDE), BF),
            pltpu.SMEM(fresh_slot.shape, jnp.int32),
            pltpu.SMEM(lengths.shape, jnp.int32),
            pltpu.SMEM(positions.shape, jnp.int32),
            pltpu.VMEM(query_latent.shape, BF),
            pltpu.VMEM((chunks, depth // chunks, heads * HEAD), BF),
            pltpu.VMEM((heads, NOPE, LAT), BF),
            pltpu.VMEM(freqs.shape, F32),
            pltpu.SemaphoreType.DMA((chunks + 6,)),
        ],
        compiler_params=params(16),
        name="project",
    )(*map(in_hbm, (fresh_slot, lengths, positions, query_latent, w_query, w_key_up, freqs)))

    own_out, own_stat, order = pl.pallas_call(
        functools.partial(own_keys_kernel, slots),
        out_shape=(
            shape((rows * piece, LAT), F32),
            shape((rows * piece, 256), F32),
            shape((32, rows * piece), BF),
        ),
        in_specs=[SMEM] * 2 + [VMEM] * 3,
        out_specs=[VMEM] * 3,
        scratch_shapes=[pltpu.VMEM((32, LAT + ROPE), F32)],
        compiler_params=params(32),
        name="own_keys",
    )(fresh_slot, positions, new_latent, freqs, own_q)

    def exchange(x, axes, n):
        return lax.all_to_all(x.reshape(n, -1, WIDE), axes, 0, 0, tiled=True).reshape(-1, WIDE)

    def swap(x):
        return lax.ppermute(x, "core", [(0, 1), (1, 0)])

    def turned(x, k, sign):
        pairs = []
        for i in range(copies):
            pairs += [(2 * i, 2 * ((i + sign * k) % copies)), (2 * i + 1, 2 * ((i - sign * k) % copies) + 1)]
        return lax.ppermute(x, ("zx", "core"), pairs)

    new_own = exchange(out_q, ("group", "zx"), slots * copies)
    res_sib = swap(res_q)
    res_both = jnp.concatenate([res_q, res_sib], 0)
    turns = sorted(range(1, copies // 2), key=lambda k: (k + 1) % 2 * copies - k)
    near = [turned(res_both, k, 1) for k in turns]
    across = turned(res_q, copies // 2, 1)
    new_own, across, *near = lax.optimization_barrier((new_own, across, *near))
    new_other = swap(new_own)
    far = swap(jnp.concatenate([*near, across], 0))
    first = 2
    first_keys = pl.pallas_call(
        fetch_kernel,
        out_shape=pltpu.VMEM((first, *fresh.shape[1:]), BF),
        in_specs=[ANY] * 2,
        out_specs=ANY,
        scratch_shapes=[pltpu.SemaphoreType.DMA],
        compiler_params=params(2),
        cost_estimate=cost(0, 4 * first * fresh[0].size),
        name="fetch_keys",
    )(new_own, in_hbm(fresh))

    send, keep, stat = pl.pallas_call(
        functools.partial(attend_kernel, piece),
        out_shape=(shape((rows * half, WIDE), BF), shape((rows * half, LAT), F32), shape((rows * half, 128), BF)),
        in_specs=[ANY] + [VMEM] * (8 + len(near)),
        out_specs=[VMEM] * 3,
        scratch_shapes=[
            pltpu.VMEM((slots - first, LAT + ROPE, tokens), BF),
            pltpu.SemaphoreType.DMA((slots - first,)),
        ],
        compiler_params=params(24),
        cost_estimate=cost(rows * 5 * 10**8, rows * 2 * 10**6),
        name="attend",
    )(in_hbm(fresh), in_vmem(first_keys), in_vmem(cache), new_own, new_other, far, res_sib, *near, across, res_q)

    new_part, *res_parts = pl.pallas_call(
        functools.partial(join_kernel, slots, piece),
        out_shape=(shape((slots * half, WIDE), BF),)
        + (shape((2 * resident * piece, WIDE), BF),) * len(near)
        + (shape((resident * piece, WIDE), BF),) * 2,
        in_specs=[VMEM] * 3,
        out_specs=(ANY,) + (VMEM,) * (len(near) + 2),
        scratch_shapes=[pltpu.VMEM((slots * half, WIDE), BF), pltpu.SemaphoreType.DMA((4,))],
        compiler_params=params(32),
        name="join_cores",
    )(swap(send), keep, stat)
    new_back = exchange(new_part, ("group", "zx"), slots * copies)
    *near, across, res_here = res_parts
    near = [turned(x, k, -1) for k, x in zip(turns, near)]
    across = turned(across, copies // 2, -1)
    own_out, own_stat, order, across, *near = lax.optimization_barrier((own_out, own_stat, order, across, *near))
    far = swap(jnp.concatenate([x[resident * piece :] for x in near], 0))
    res_back = [res_here, across, *near, far]

    new_out = pl.pallas_call(
        functools.partial(finish_new_kernel, slots),
        out_shape=shape((32, heads * 128), F32),
        in_specs=[VMEM] * 5,
        out_specs=VMEM,
        compiler_params=params(32),
        cost_estimate=cost(4 * 10**8, 2 * 10**6),
        name="finish_new",
    )(order, new_back, own_out, own_stat, w_value_up)

    return pl.pallas_call(
        functools.partial(finish_resident_kernel, slots),
        out_shape=shape((rows, 2, heads * 128), BF),
        in_specs=[VMEM] * (5 + len(res_back)),
        out_specs=VMEM,
        compiler_params=params(32),
        name="finish",
    )(order, own_out, own_stat, w_value_up, new_out, *res_back)


def solution(mesh):
    groups, shards = mesh.devices.shape
    split = Mesh(mesh.devices.reshape(groups, shards // 2, 2), ("group", "zx", "core"))
    ctx = ("zx", "core")
    placed = (
        P("group", None, None),
        P(None, ctx),
        P(ctx, None, None),
        P(ctx, None, None),
        P("group", ctx, None),
        P("group", None, ctx, None),
        P("group", None, None),
        P("group"),
        P("group", None),
        P("group", None),
    )
    return jax.shard_map(
        local, mesh=split, in_specs=placed, out_specs=P("group", None, ctx), check_vma=False
    )
```

```python
import functools
import math

import jax
import jax.numpy as jnp
import numpy as np
from jax import lax
from jax.experimental import pallas as pl
from jax.experimental.pallas import tpu as pltpu
from jax.sharding import Mesh
from jax.sharding import PartitionSpec as P

LAT = 512
ROPE = 64
NOPE = 128
HEAD = NOPE + ROPE
WIDE = 640
SCALE = HEAD ** (-0.5)
NONE = -1e30
BF = jnp.bfloat16
F32 = jnp.float32

HALF_PI = (1.5703125, 0.0004825592041015625, 1.2676710047e-06)


def dot(a, b, contract=((1,), (0,))):
    return lax.dot_general(a, b, (contract, ((), ())), preferred_element_type=F32)


def iota(shape, dim):
    return lax.broadcasted_iota(jnp.int32, shape, dim)


def cos_sin(angle):
    turns = jnp.floor(angle * (2.0 / math.pi) + 0.5)
    rest = angle - turns * HALF_PI[0]
    rest = rest - turns * HALF_PI[1]
    rest = rest - turns * HALF_PI[2]
    sq = rest * rest
    sine = rest + rest * sq * (
        -1.6666654611e-1 + sq * (8.3321608736e-3 + sq * -1.9515295891e-4)
    )
    cosine = 1.0 - 0.5 * sq + sq * sq * (
        4.166664568298827e-2 + sq * (-1.388731625493765e-3 + sq * 2.443315711809948e-5)
    )
    quarter = turns.astype(jnp.int32) & 3
    swapped = (quarter & 1) == 1
    first = jnp.where(swapped, sine, cosine)
    second = jnp.where(swapped, cosine, sine)
    first = jnp.where((quarter == 1) | (quarter == 2), -first, first)
    second = jnp.where(quarter >= 2, -second, second)
    return first, second


def rope(values, cosine, signed_sine):
    half = ROPE // 2
    swapped = jnp.concatenate([values[:, half:], values[:, :half]], 1)
    return values * cosine + swapped * signed_sine


def per_row(get, rows, width):
    at = iota((32, 1), 0)
    out = jnp.zeros((32, 1), jnp.int32)
    for r in range(rows):
        for s in range(width):
            out = jnp.where(at // (2 // width) == r * width + s, get(r, s), out)
    return out


def angles_of(pos_ref, freq_ref, rows):
    at = per_row(lambda r, s: pos_ref[s, r], rows, 2).astype(F32)
    cosine, sine = cos_sin(at * freq_ref[...])
    signed = jnp.where(iota((1, ROPE), 1) < ROPE // 2, -1.0, 1.0) * sine
    return cosine, signed


def row_of(slot_ref, slots, resident, shape, dim, per):
    at = iota(shape, dim)
    slot = at // per
    out = slot - slots
    for j in range(slots):
        out = jnp.where(slot == slot_ref[0, j], resident + j, out)
    return out


def project_kernel(heads, slots, copies, slot_hbm, len_hbm, pos_hbm, ql_hbm, wq_hbm, wk_hbm, freq_hbm,
                   out_ref, res_ref, own_ref, rows_ref, all_ref, slot_ref, len_ref, pos_ref, ql_ref, wq_ref, wk_ref,
                   freq_ref, sems):
    rows = ql_ref.shape[0]
    resident = rows - slots
    chunks = wq_ref.shape[0]
    step = wq_ref.shape[1]
    small = ((ql_hbm, ql_ref), (slot_hbm, slot_ref), (len_hbm, len_ref), (pos_hbm, pos_ref), (freq_hbm, freq_ref))
    small = [pltpu.make_async_copy(*pair, sems.at[chunks + 1 + n]) for n, pair in enumerate(small)]
    loads = [
        pltpu.make_async_copy(wq_hbm.at[pl.ds(c * step, step)], wq_ref.at[c], sems.at[c]) for c in range(chunks)
    ]
    loads.append(pltpu.make_async_copy(wk_hbm, wk_ref, sems.at[chunks]))
    for load in small + loads:
        load.start()
    for load in small:
        load.wait()
    rows_ref[...] = jnp.zeros_like(rows_ref)
    for r in range(rows):
        rows_ref[2 * r : 2 * r + 2, :] = ql_ref[r].astype(F32)
    cosine, signed = angles_of(pos_ref, freq_ref, rows)
    length = per_row(lambda r, s: len_ref[r], rows, 1)
    lane = iota((1, WIDE - LAT - ROPE), 1)
    meta = jnp.where(lane == 0, (length // 128).astype(F32), jnp.where(lane == 1, (length % 128).astype(F32), 0.0))
    piece = 2 * heads
    count = rows * piece
    row = row_of(slot_ref, slots, resident, (count, 1), 0, piece)
    inner = iota((count, 1), 0) % piece
    source = (inner // 2) * 32 + 2 * row + inner % 2
    select = jnp.where(iota((count, heads * 32), 1) == source, 1.0, 0.0).astype(BF)
    qfull = 0.0
    for c in range(chunks):
        loads[c].wait()
        qfull = qfull + dot(rows_ref[:, c * step : (c + 1) * step].astype(BF), wq_ref[c])
    qfull = qfull.astype(BF)
    loads[chunks].wait()
    for h in range(heads):
        part = qfull[:, h * HEAD : (h + 1) * HEAD]
        all_ref[h * 32 : (h + 1) * 32, :LAT] = dot(part[:, :NOPE], wk_ref[h]).astype(BF)
        tail = jnp.concatenate([rope(part[:, NOPE:].astype(F32), cosine, signed), meta], 1)
        all_ref[h * 32 : (h + 1) * 32, LAT:] = tail.astype(BF)
    own = dot(select, all_ref[...])
    own_ref[...] = own.astype(BF)
    for p in range(slots):
        one = own[p * piece : (p + 1) * piece]
        two = jnp.concatenate([one, one], 0).astype(BF)
        for k in range(0, copies, 2):
            at = (p * copies + k) * piece
            out_ref[at : at + 2 * piece, :] = two
    res_ref[...] = own[slots * piece :].astype(BF)


def own_keys_kernel(slots, slot_ref, pos_ref, nl_ref, freq_ref, own_ref, out_ref, stat_ref, order_ref, keys_ref):
    rows = nl_ref.shape[0]
    resident = rows - slots
    count = own_ref.shape[0]
    piece = count // rows
    keys_ref[...] = jnp.zeros_like(keys_ref)
    for r in range(rows):
        keys_ref[2 * r : 2 * r + 2, :] = nl_ref[r].astype(F32)
    cosine, signed = angles_of(pos_ref, freq_ref, rows)
    latent = keys_ref[:, :LAT].astype(BF)
    turned = rope(keys_ref[:, LAT:], cosine, signed).astype(BF)
    scores = dot(own_ref[:, :LAT], latent, ((1,), (1,)))
    scores = scores + dot(own_ref[:, LAT : LAT + ROPE], turned, ((1,), (1,)))
    scores = scores * SCALE
    row = row_of(slot_ref, slots, resident, (count, 1), 0, piece)
    step = iota((count, 1), 0) % 2
    key = iota((1, 32), 1)
    allowed = (key // 2 == row) & (key % 2 <= step)
    highest = jnp.max(jnp.where(allowed, scores, NONE), 1, keepdims=True)
    weights = jnp.where(allowed, jnp.exp(scores - highest), 0.0)
    total = jnp.sum(weights, 1, keepdims=True)
    out_ref[...] = dot(weights.astype(BF), latent)
    stat_ref[:, :128] = jnp.broadcast_to(highest, (count, 128))
    stat_ref[:, 128:] = jnp.broadcast_to(total, (count, 128))
    row = row_of(slot_ref, slots, resident, (1, count), 1, piece)
    target = 2 * row + iota((1, count), 1) % 2
    order_ref[...] = jnp.where(iota((32, count), 0) == target, 1.0, 0.0).astype(BF)


def parts_of(value):
    first = value.astype(BF).astype(F32)
    second = (value - first).astype(BF).astype(F32)
    return first, second, value - first - second


def with_stats(highest, total):
    lane = iota((1, 128), 1)
    out = 0.0
    for at, part in enumerate(parts_of(highest) + parts_of(total)):
        out = jnp.where(lane == at, part, out)
    return out.astype(BF)


def stats_of(tail):
    at = iota((128, 256), 0)
    pick = jnp.where((at < 6) & (at // 3 == iota((128, 256), 1) // 128), 1.0, 0.0).astype(BF)
    both = dot(tail, pick)
    return both[:, :128], both[:, 128:]


def spread(value):
    return jnp.concatenate([value] * (LAT // 128), -1)


def softmax_part(scores, length):
    scores = jnp.where(iota((1, scores.shape[1]), 1) < length, scores, NONE)
    highest = jnp.max(scores, 1, keepdims=True)
    weights = jnp.exp((scores - jnp.maximum(highest, 0.1 * NONE)) * SCALE)
    return highest * SCALE, jnp.sum(weights, 1, keepdims=True), weights.astype(BF)


def fetch_kernel(after_hbm, fresh_hbm, keys_ref, sem):
    load = pltpu.make_async_copy(fresh_hbm.at[pl.ds(0, keys_ref.shape[0])], keys_ref, sem)
    load.start()
    load.wait()


def attend_kernel(piece, fresh_hbm, first_ref, cache_ref, new_own, new_other, *refs):
    send_ref, keep_ref, stat_ref, keys_ref, sems = refs[-5:]
    blocks = refs[:-5]
    res_other, res_own = blocks[:2], blocks[2:]
    slots, resident = fresh_hbm.shape[0], cache_ref.shape[0]
    rows = slots + resident
    half = new_own.shape[0] // slots
    here = first_ref.shape[0]
    loads = [pltpu.make_async_copy(fresh_hbm.at[here + i], keys_ref.at[i], sems.at[i]) for i in range(slots - here)]
    for load in loads:
        load.start()
    offset = (lax.axis_index("zx") * lax.axis_size("core") + lax.axis_index("core")) * keys_ref.shape[2]

    def queries_of(i):
        if i < slots:
            span = slice(i * half, (i + 1) * half)
            return jnp.concatenate([new_other[span, :], new_own[span, :]], 0)
        at = (i - slots) * piece
        step = resident * piece
        return jnp.concatenate(
            [ref[k + at : k + at + piece, :] for ref in res_other + res_own for k in range(0, ref.shape[0], step)], 0
        )

    def keys_of(i):
        if i < here:
            return first_ref.at[i]
        return keys_ref.at[i - here] if i < slots else cache_ref.at[i - slots]

    def scores_of(i):
        queries = queries_of(i)
        length = queries[:, LAT + ROPE : LAT + ROPE + 2].astype(F32)
        length = (length[:, 0:1] * 128.0 + length[:, 1:2]).astype(jnp.int32) - offset
        return dot(queries[:, : LAT + ROPE], keys_of(i)[...]), length

    order = [*range(slots, rows), *range(slots)]
    arrived = here
    ahead = scores_of(order[0])
    for n, i in enumerate(order):
        scores, length = ahead
        if n + 1 < rows:
            if order[n + 1] == arrived:
                upto = min(slots, arrived + 3)
                for load in loads[arrived - here : upto - here]:
                    load.wait()
                arrived = upto
            ahead = scores_of(order[n + 1])
        highest, total, weights = softmax_part(scores, length)
        mean = dot(weights, keys_of(i)[:LAT, :], ((1,), (1,))) * (1.0 / jnp.maximum(total, 1e-30))
        stats = with_stats(highest, total)
        span = slice(i * half, (i + 1) * half)
        send_ref[span, :LAT] = mean[:half].astype(BF)
        send_ref[span, LAT:] = stats[:half]
        keep_ref[span, :] = mean[half:]
        stat_ref[span, :] = stats[half:]


def joined(got, keep, stat):
    far_highest, far_total = stats_of(got[:, LAT:])
    highest, total = stats_of(stat)
    top = jnp.maximum(far_highest, highest)
    far_total = far_total * jnp.exp(far_highest - top)
    total = total * jnp.exp(highest - top)
    both = total + far_total
    scale = 1.0 / jnp.maximum(both, 1e-30)
    mean = got[:, :LAT].astype(F32) * spread(far_total * scale) + keep * spread(total * scale)
    return mean.astype(BF), with_stats(top, both)


def join_kernel(slots, piece, got_ref, keep_ref, stat_ref, new_hbm, *refs):
    res_refs, new_ref, sems = refs[:-2], refs[-2], refs[-1]
    count = new_ref.shape[0]
    half = count // slots
    resident = got_ref.shape[0] // half - slots
    parts = sems.shape[0]
    stores = []
    for c in range(parts):
        span = slice(c * count // parts, (c + 1) * count // parts)
        mean, stats = joined(got_ref[span, :], keep_ref[span, :], stat_ref[span, :])
        new_ref[span, :LAT] = mean
        new_ref[span, LAT:] = stats
        at = pl.ds(c * count // parts, count // parts)
        stores.append(pltpu.make_async_copy(new_ref.at[at], new_hbm.at[at], sems.at[c]))
        stores[c].start()
    mean, stats = joined(got_ref[count:, :], keep_ref[count:, :], stat_ref[count:, :])
    block = 0
    for ref in res_refs:
        for k in range(0, ref.shape[0], resident * piece):
            for i in range(resident):
                at = i * half + block * piece
                span = slice(k + i * piece, k + (i + 1) * piece)
                ref[span, :LAT] = mean[at : at + piece]
                ref[span, LAT:] = stats[at : at + piece]
            block += 1
    for store in stores:
        store.wait()


def merged(means, tails, own, own_highest, own_total):
    copies, n = means.shape[:2]
    highest, total = (x.reshape(copies, n, 128) for x in stats_of(tails.reshape(copies * n, 128)))
    top = jnp.maximum(jnp.max(highest, 0), own_highest)
    share = total * jnp.exp(highest - top[None])
    own_fade = jnp.exp(own_highest - top)
    scale = 1.0 / (jnp.sum(share, 0) + own_total * own_fade)
    summed = own * spread(own_fade * scale)
    share = share * scale[None]
    for k in range(copies):
        summed = summed + means[k].astype(F32) * spread(share[k])
    return summed.astype(BF)


def raised(latent, wv_ref, order):
    heads = wv_ref.shape[0]
    head = iota((latent.shape[0], 1), 0) % (2 * heads) // 2
    values = [jnp.where(head == h, dot(latent, wv_ref[h]), 0.0).astype(BF) for h in range(heads)]
    return dot(order, jnp.concatenate(values, 1))


def finish_new_kernel(slots, order_ref, new_ref, own_ref, stat_ref, wv_ref, out_ref):
    piece = 2 * wv_ref.shape[0]
    half = new_ref.shape[0] // slots
    latent = []
    for p in range(slots):
        block = new_ref[p * half : (p + 1) * half, :].reshape(half // piece, piece, WIDE)
        span = slice(p * piece, (p + 1) * piece)
        own = own_ref[span, :], stat_ref[span, :128], stat_ref[span, 128:]
        latent.append(merged(block[..., :LAT], block[..., LAT:], *own))
    out_ref[...] = raised(jnp.concatenate(latent, 0), wv_ref, order_ref[:, : slots * piece])


def finish_resident_kernel(slots, order_ref, own_ref, stat_ref, wv_ref, new_ref, *refs):
    *near_refs, far_ref, out_ref = refs
    rows = out_ref.shape[0]
    piece = 2 * wv_ref.shape[0]
    n = (rows - slots) * piece
    parts = [ref[:n, :] for ref in near_refs] + [far_ref[k : k + n, :] for k in range(0, far_ref.shape[0], n)]
    block = jnp.stack(parts)
    span = slice(slots * piece, rows * piece)
    own = own_ref[span, :], stat_ref[span, :128], stat_ref[span, 128:]
    latent = merged(block[..., :LAT], block[..., LAT:], *own)
    out = new_ref[...] + raised(latent, wv_ref, order_ref[:, slots * piece :])
    for r in range(rows):
        out_ref[r] = out[2 * r : 2 * r + 2].astype(BF)


VMEM = pl.BlockSpec(memory_space=pltpu.VMEM)
SMEM = pl.BlockSpec(memory_space=pltpu.SMEM)
ANY = pl.BlockSpec(memory_space=pl.ANY)


def shape(dims, dtype):
    return jax.ShapeDtypeStruct(dims, dtype)


def params(mebibytes):
    return pltpu.CompilerParams(vmem_limit_bytes=mebibytes * 1024 * 1024)


def cost(flops, moved):
    return pl.CostEstimate(flops=flops, bytes_accessed=moved, transcendentals=0)


def local(query_latent, w_query, w_key_up, w_value_up, cache, fresh, new_latent, lengths, fresh_slot, positions):
    rows, _, depth = query_latent.shape
    heads = w_key_up.shape[0]
    slots = fresh_slot.shape[1]
    resident = rows - slots
    tokens = cache.shape[1]
    copies = lax.axis_size("zx")
    piece = 2 * heads
    half = copies * piece
    chunks = 6
    freqs = 50000.0 ** (-np.arange(ROPE // 2, dtype=np.float64) / (ROPE // 2))
    freqs = jnp.asarray(np.concatenate([freqs, freqs]).astype(np.float32)[None])
    positions = positions.T
    cache = jnp.swapaxes(cache, 1, 2)
    fresh = jnp.swapaxes(fresh[0], 1, 2)

    def in_vmem(x):
        return pltpu.with_memory_space_constraint(x, pltpu.VMEM)

    def in_hbm(x):
        return pltpu.with_memory_space_constraint(x, pltpu.HBM)

    out_q, res_q, own_q = pl.pallas_call(
        functools.partial(project_kernel, heads, slots, copies),
        out_shape=(
            shape((slots * half, WIDE), BF),
            shape((resident * piece, WIDE), BF),
            shape((rows * piece, WIDE), BF),
        ),
        in_specs=[ANY] * 7,
        out_specs=[VMEM] * 3,
        scratch_shapes=[
            pltpu.VMEM((32, depth), F32),
            pltpu.VMEM((heads * 32, WIDE), BF),
            pltpu.SMEM(fresh_slot.shape, jnp.int32),
            pltpu.SMEM(lengths.shape, jnp.int32),
            pltpu.SMEM(positions.shape, jnp.int32),
            pltpu.VMEM(query_latent.shape, BF),
            pltpu.VMEM((chunks, depth // chunks, heads * HEAD), BF),
            pltpu.VMEM((heads, NOPE, LAT), BF),
            pltpu.VMEM(freqs.shape, F32),
            pltpu.SemaphoreType.DMA((chunks + 6,)),
        ],
        compiler_params=params(16),
        name="project",
    )(*map(in_hbm, (fresh_slot, lengths, positions, query_latent, w_query, w_key_up, freqs)))

    own_out, own_stat, order = pl.pallas_call(
        functools.partial(own_keys_kernel, slots),
        out_shape=(
            shape((rows * piece, LAT), F32),
            shape((rows * piece, 256), F32),
            shape((32, rows * piece), BF),
        ),
        in_specs=[SMEM] * 2 + [VMEM] * 3,
        out_specs=[VMEM] * 3,
        scratch_shapes=[pltpu.VMEM((32, LAT + ROPE), F32)],
        compiler_params=params(32),
        name="own_keys",
    )(fresh_slot, positions, new_latent, freqs, own_q)

    def exchange(x, axes, n):
        return lax.all_to_all(x.reshape(n, -1, WIDE), axes, 0, 0, tiled=True).reshape(-1, WIDE)

    def swap(x):
        return lax.ppermute(x, "core", [(0, 1), (1, 0)])

    def turned(x, k, sign):
        pairs = []
        for i in range(copies):
            pairs += [(2 * i, 2 * ((i + sign * k) % copies)), (2 * i + 1, 2 * ((i - sign * k) % copies) + 1)]
        return lax.ppermute(x, ("zx", "core"), pairs)

    new_own = exchange(out_q, ("group", "zx"), slots * copies)
    res_sib = swap(res_q)
    res_both = jnp.concatenate([res_q, res_sib], 0)
    turns = sorted(range(1, copies // 2), key=lambda k: (k + 1) % 2 * copies - k)
    near = [turned(res_both, k, 1) for k in turns]
    across = turned(res_q, copies // 2, 1)
    new_own, across, *near = lax.optimization_barrier((new_own, across, *near))
    new_other = swap(new_own)
    far = swap(jnp.concatenate([*near, across], 0))
    first = 2
    first_keys = pl.pallas_call(
        fetch_kernel,
        out_shape=pltpu.VMEM((first, *fresh.shape[1:]), BF),
        in_specs=[ANY] * 2,
        out_specs=ANY,
        scratch_shapes=[pltpu.SemaphoreType.DMA],
        compiler_params=params(2),
        cost_estimate=cost(0, 4 * first * fresh[0].size),
        name="fetch_keys",
    )(new_own, in_hbm(fresh))

    send, keep, stat = pl.pallas_call(
        functools.partial(attend_kernel, piece),
        out_shape=(shape((rows * half, WIDE), BF), shape((rows * half, LAT), F32), shape((rows * half, 128), BF)),
        in_specs=[ANY] + [VMEM] * (8 + len(near)),
        out_specs=[VMEM] * 3,
        scratch_shapes=[
            pltpu.VMEM((slots - first, LAT + ROPE, tokens), BF),
            pltpu.SemaphoreType.DMA((slots - first,)),
        ],
        compiler_params=params(24),
        cost_estimate=cost(rows * 5 * 10**8, rows * 2 * 10**6),
        name="attend",
    )(in_hbm(fresh), in_vmem(first_keys), in_vmem(cache), new_own, new_other, far, res_sib, *near, across, res_q)

    new_part, *res_parts = pl.pallas_call(
        functools.partial(join_kernel, slots, piece),
        out_shape=(shape((slots * half, WIDE), BF),)
        + (shape((2 * resident * piece, WIDE), BF),) * len(near)
        + (shape((resident * piece, WIDE), BF),) * 2,
        in_specs=[VMEM] * 3,
        out_specs=(ANY,) + (VMEM,) * (len(near) + 2),
        scratch_shapes=[pltpu.VMEM((slots * half, WIDE), BF), pltpu.SemaphoreType.DMA((2,))],
        compiler_params=params(32),
        name="join_cores",
    )(swap(send), keep, stat)
    new_back = exchange(new_part, ("group", "zx"), slots * copies)
    *near, across, res_here = res_parts
    near = [turned(x, k, -1) for k, x in zip(turns, near)]
    across = turned(across, copies // 2, -1)
    own_out, own_stat, order, across, *near = lax.optimization_barrier((own_out, own_stat, order, across, *near))
    far = swap(jnp.concatenate([x[resident * piece :] for x in near], 0))
    res_back = [res_here, across, *near, far]

    new_out = pl.pallas_call(
        functools.partial(finish_new_kernel, slots),
        out_shape=shape((32, heads * 128), F32),
        in_specs=[VMEM] * 5,
        out_specs=VMEM,
        compiler_params=params(32),
        cost_estimate=cost(4 * 10**8, 2 * 10**6),
        name="finish_new",
    )(order, new_back, own_out, own_stat, w_value_up)

    return pl.pallas_call(
        functools.partial(finish_resident_kernel, slots),
        out_shape=shape((rows, 2, heads * 128), BF),
        in_specs=[VMEM] * (5 + len(res_back)),
        out_specs=VMEM,
        compiler_params=params(32),
        name="finish",
    )(order, own_out, own_stat, w_value_up, new_out, *res_back)


def solution(mesh):
    groups, shards = mesh.devices.shape
    split = Mesh(mesh.devices.reshape(groups, shards // 2, 2), ("group", "zx", "core"))
    ctx = ("zx", "core")
    placed = (
        P("group", None, None),
        P(None, ctx),
        P(ctx, None, None),
        P(ctx, None, None),
        P("group", ctx, None),
        P("group", None, ctx, None),
        P("group", None, None),
        P("group"),
        P("group", None),
        P("group", None),
    )
    return jax.shard_map(
        local, mesh=split, in_specs=placed, out_specs=P("group", None, ctx), check_vma=False
    )
```
